32 devices in a mesh: groups: 2 (over x), tensor: 8 (over z, y), replica: 2 (over core).
Axes of the slice: x: 2, y: 2, z: 4, core: 2. Of those that a mesh axis runs over, the one named last changes fastest.
Arguments:
- inputs: bfloat16 [2048, 8192], P(('groups', 'replica'), 'tensor'), parts along dimension 0, may hold values from -34 to 34, as said below
- entry_gain: bfloat16 [8192], replicated, may hold values from 0.099609375 to 1.8984375
- exit_gain: bfloat16 [8192], replicated, may hold values from 0.099609375 to 1.8984375
- query_weight: bfloat16 [8192, 8192], P(None, 'tensor'), may hold values from -0.0625 to 0.0625
- key_value_matrix: bfloat16 [8192, 2048], P('tensor'), may hold values from -0.0625 to 0.0625
- output_weight: bfloat16 [8192, 8192], P('tensor'), may hold values from -0.09375 to 0.09375
- page_pool: bfloat16 [384, 16, 2048], P(('groups', 'replica')), parts along dimension 0, may hold values from -300 to 300, as said below
- page_table: int32 [1024, 4], P(('groups', 'replica')), parts along dimension 0, may hold values from 0 to 95
- positions: int32 [1024], P(('groups', 'replica')), parts along dimension 0, may hold values from 1 to 64
- request_lengths: int32 [4, 8], P(('groups', 'replica')), parts along dimension 0, may hold values from 1 to 128, 256 in all within a row
- prefix_pages: int32 [4, 8], P(('groups', 'replica')), parts along dimension 0, may hold values from 1 to 4, as said below
- source_pages: int32 [4, 8, 4], P(('groups', 'replica')), parts along dimension 0, may hold values from 0 to 95
- target_pages: int32 [4, 8, 4], P(('groups', 'replica')), parts along dimension 0, may hold values from 0 to 95, as said below
Outputs:
- hidden: bfloat16 [2048, 8192], P(('groups', 'replica'), 'tensor'), parts along dimension 0
- normed_out: bfloat16 [2048, 8192], P(('groups', 'replica'), 'tensor'), parts along dimension 0
The draws below stay inside these ranges and needn't reach their ends.
There are 2 independent parts, one for each index of `groups`. The reference program is written for one: setup_inputs(seed, part) draws one part's arguments, and reference() takes and returns one part's arrays. A program takes and returns all parts, laid end to end along the dimension named above; an argument that names none is the same for every part. Nothing has to cross between parts.
Inputs may be any that keep to these rules, and one draw needn't show every extreme that they name: `inputs`: real-valued activations. `page_pool`: real-valued cached keys and values. `prefix_pages`: in each replica some request has exactly 4 prefix pages. `target_pages`: all distinct within a replica. `request_lengths`: each replica's requests fill its 256 prefill tokens, in order.
All inputs are finite; a program needn't handle non-finite values.
Results may differ from the reference program's by a relative error of at most 0.012.
The reference program's roundings to bfloat16 on the way count: a program that leaves them out, or rounds other values in their place, can miss the bound.
Values may be sent and summed in bfloat16 or wider, within the bound.
No kernel may reach another device: no remote copies, remote signals or barrier semaphores. Data moves between devices by JAX's collectives and lax.ppermute only.
A program may use at most 192 MiB of HBM per device.

```python
import math
import jax
import jax.numpy as jnp
import numpy as np
from jax import lax

MODEL_WIDTH = 8192
QUERY_HEADS = 64
KEY_VALUE_HEADS = 8
HEAD_SIZE = 128
PRE = 256
DECODE_ROWS = 256
MOVED_REQUESTS = 8
PREFIX_PAGE_MAX = 4
PAGE_TOKENS = 16
TABLE_PAGES = 4
REPLICA_PAGES = 96
N_REPLICA = 2


def draw_inputs(key, part):
    key = jax.random.fold_in(key, 11)
    row_key, col_key, starting_key = jax.random.split(key, 3)
    rows_total = N_REPLICA * (PRE + DECODE_ROWS)
    row_scale = 10.0 ** jax.random.uniform(row_key, (rows_total, 1), jnp.float32, -0.3, 0.3)
    column = jnp.arange(MODEL_WIDTH, dtype=jnp.float32)[None, :] / MODEL_WIDTH
    col_scale = 10.0 ** (0.48 * column - 0.24 + jax.random.uniform(col_key, (1, MODEL_WIDTH), jnp.float32, -0.2, 0.2))
    starting_sample = jnp.clip(jax.random.normal(starting_key, (rows_total, MODEL_WIDTH), jnp.float32), -6.0, 6.0)
    return (starting_sample * row_scale * col_scale).astype(jnp.bfloat16)


def draw_page_pool(key, part):
    key = jax.random.fold_in(key, 23)
    starting_key = jax.random.fold_in(key, 0)
    starting_sample = jnp.clip(jax.random.normal(starting_key, (N_REPLICA * REPLICA_PAGES, PAGE_TOKENS, KEY_VALUE_HEADS * 2 * HEAD_SIZE), jnp.float32), -6.0, 6.0)
    return starting_sample.astype(jnp.bfloat16)


def draw_prefix_pages(key, part):
    key = jax.random.fold_in(key, 37)
    count_key, pick_key = jax.random.split(key)
    counts = jax.random.randint(count_key, (N_REPLICA, MOVED_REQUESTS), 1, PREFIX_PAGE_MAX + 1)
    chosen = jax.random.randint(pick_key, (N_REPLICA, 1), 0, MOVED_REQUESTS)
    return jnp.where(jnp.arange(MOVED_REQUESTS)[None, :] == chosen, PREFIX_PAGE_MAX, counts).astype(jnp.int32)


def pick_pages(one_key):
    return jax.random.permutation(one_key, REPLICA_PAGES)[:MOVED_REQUESTS * PREFIX_PAGE_MAX]


def draw_target_pages(key, part):
    key = jax.random.fold_in(key, 53)
    replica_keys = jax.random.split(key, N_REPLICA)
    picked = jax.vmap(pick_pages)(replica_keys)
    return picked.reshape(N_REPLICA, MOVED_REQUESTS, PREFIX_PAGE_MAX).astype(jnp.int32)


def touch_ends(drawn, key, smallest, largest):
    extent = drawn.shape
    index_at = [jax.random.randint(jax.random.fold_in(key, axis), (), 0, extent[axis]) for axis in range(len(extent))]
    drawn = drawn.at[tuple(index_at)].set(smallest)
    longest = extent.index(max(extent))
    index_at[longest] = (index_at[longest] + 1) % extent[longest]
    return drawn.at[tuple(index_at)].set(largest)


def strengthened(entries, own_key, source, target, blocks, factor):
    owner, partner = [(jnp.arange(entries.shape[position]) // (entries.shape[position] // blocks)).reshape([-1 if axis == position else 1 for axis in range(entries.ndim)]) for position in (source, target)]
    chosen = jax.random.permutation(own_key, blocks)[partner]
    strong = (owner == chosen) | (owner == (partner + blocks // 2) % blocks)
    return jnp.where(strong, factor * entries, entries)


def levels(rng, shape, cuts, smallest, high):
    factor_of = 1.0
    for axis_at, blocks in cuts:
        heights = jax.random.uniform(jax.random.fold_in(jax.random.fold_in(rng, 6), axis_at), (blocks,), jnp.float32, smallest / len(cuts), high / len(cuts))
        factor_of = factor_of * jnp.repeat(jnp.exp(heights), shape[axis_at] // blocks).reshape((-1,) + (1,) * (len(shape) - 1 - axis_at))
    return factor_of


def split_up(count, total, limit, skew):
    portions = [(1 << 20) // math.isqrt(rank ** skew) + 1 for rank in range(2, count + 1)]
    spare, given = total - limit - (count - 1), [1] * (count - 1)
    while spare > 0:
        candidates = [i for i in range(count - 1) if given[i] < limit]
        mass, budget = sum([portions[i] for i in candidates]), spare
        for i in candidates:
            extra = min(limit - given[i], max(1, budget * portions[i] // mass), spare)
            given[i] = given[i] + extra
            spare = spare - extra
    return np.array([limit] + given)


def uneven_parts(own_key, number_of, total, bound, skew):
    if number_of == 2:
        one = jax.random.randint(own_key, (), max(1, total - bound), min(bound, total - 1) + 1)
        return jnp.stack([one, total - one])
    sizes = jnp.asarray(split_up(number_of, total, bound, skew), jnp.int32)
    twos = (number_of - 1) // 2
    giver, sink = sizes[1:1 + 2 * twos:2], sizes[2:2 + 2 * twos:2]
    margin = jnp.minimum(giver - 1, bound - sink)
    shifted = jax.random.randint(jax.random.fold_in(own_key, 1), (twos,), 0, 1 << 20) % (margin + 1)
    sizes = sizes.at[1:1 + 2 * twos:2].set(giver - shifted).at[2:2 + 2 * twos:2].set(sink + shifted)
    return sizes[jax.random.permutation(jax.random.fold_in(own_key, 2), number_of)]


def bell_draw(own_key, dims, scale, reach, cuts=(), held_as=jnp.bfloat16):
    loudness = levels(own_key, dims, cuts, -0.22, 0.18) if cuts else 1.0
    values = jax.random.normal(own_key, dims, jnp.float32) * scale * loudness
    return jnp.minimum(jnp.maximum(values, -reach), reach).astype(held_as)


def bell_draw_with(stream_key, extent, deviation, limit, cuts, heavy, held_as=jnp.bfloat16):
    entries = deviation * jax.random.normal(stream_key, extent, jnp.float32)
    if cuts:
        entries = entries * levels(stream_key, extent, cuts, -0.22, 0.18)
    return jnp.clip(strengthened(entries, jax.random.fold_in(stream_key, 3), *heavy), -limit, limit).astype(held_as)


def setup_inputs(seed: int = 0, part: int = 0) -> dict:
    keys = jax.random.split(jax.random.key(seed), 14)
    own_keys = jax.random.split(jax.random.fold_in(keys[13], part), 14)
    inputs = draw_inputs(jax.random.fold_in(jax.random.fold_in(keys[13], part), 71), part)
    entry_gain = jnp.clip(1.0 + 0.18 * jax.random.normal(keys[1], (MODEL_WIDTH,), jnp.float32), 0.099609375, 1.8984375).astype(jnp.bfloat16)
    exit_gain = jnp.clip(1.0 + 0.18 * jax.random.normal(keys[2], (MODEL_WIDTH,), jnp.float32), 0.099609375, 1.8984375).astype(jnp.bfloat16)
    query_weight = bell_draw(keys[3], (MODEL_WIDTH, QUERY_HEADS * HEAD_SIZE), MODEL_WIDTH ** -0.5, 0.0625, ((1, 8),))
    key_value_matrix = bell_draw(keys[4], (MODEL_WIDTH, KEY_VALUE_HEADS * 2 * HEAD_SIZE), MODEL_WIDTH ** -0.5, 0.0625, ((0, 8),))
    output_weight = bell_draw_with(keys[5], (QUERY_HEADS * HEAD_SIZE, MODEL_WIDTH), (QUERY_HEADS * HEAD_SIZE) ** -0.5, 0.09375, ((0, 8),), (0, 1, 8, 2.0))
    page_pool = draw_page_pool(jax.random.fold_in(jax.random.fold_in(keys[13], part), 71), part)
    page_table = touch_ends(jax.random.randint(own_keys[7], (N_REPLICA * DECODE_ROWS, TABLE_PAGES), 0, REPLICA_PAGES), jax.random.fold_in(own_keys[7], 1), 0, REPLICA_PAGES - 1).astype(jnp.int32)
    positions = touch_ends(jax.random.randint(own_keys[8], (N_REPLICA * DECODE_ROWS,), 1, TABLE_PAGES * PAGE_TOKENS + 1), jax.random.fold_in(own_keys[8], 1), 1, TABLE_PAGES * PAGE_TOKENS).astype(jnp.int32)
    request_lengths = jax.vmap(lambda own: uneven_parts(own, MOVED_REQUESTS, PRE, PRE // 2, 2))(jax.random.split(own_keys[9], N_REPLICA)).reshape((N_REPLICA, MOVED_REQUESTS)).astype(jnp.int32)
    prefix_pages = draw_prefix_pages(jax.random.fold_in(jax.random.fold_in(keys[13], part), 71), part)
    source_pages = touch_ends(jax.random.randint(own_keys[11], (N_REPLICA, MOVED_REQUESTS, PREFIX_PAGE_MAX), 0, REPLICA_PAGES), jax.random.fold_in(own_keys[11], 1), 0, REPLICA_PAGES - 1).astype(jnp.int32)
    target_pages = draw_target_pages(jax.random.fold_in(jax.random.fold_in(keys[13], part), 71), part)
    return {"inputs": inputs, "entry_gain": entry_gain, "exit_gain": exit_gain, "query_weight": query_weight, "key_value_matrix": key_value_matrix, "output_weight": output_weight, "page_pool": page_pool, "page_table": page_table, "positions": positions, "request_lengths": request_lengths, "prefix_pages": prefix_pages, "source_pages": source_pages, "target_pages": target_pages}


EPS = 1e-06
THETA = 1000000.0
NEGATIVE = -1e+30

def norm_rows(values, gain):
    inv_norm = lax.rsqrt(lax.optimization_barrier(jnp.mean(values * values, axis=-1, keepdims=True)) + EPS)
    return values * inv_norm * gain.astype(jnp.float32)

def rotate(values, positions):
    half_dim = values.shape[-1] // 2
    frequency = jnp.exp(jnp.arange(half_dim, dtype=jnp.float32) * (-2.0 * math.log(THETA) / values.shape[-1]))
    angles = positions.astype(jnp.float32)[:, None] * frequency[None, :]
    cosine = jnp.cos(angles)[:, None, :]
    sine_part = jnp.sin(angles)[:, None, :]
    first_half = values[..., :half_dim]
    second = values[..., half_dim:]
    return jnp.concatenate([first_half * cosine - second * sine_part, second * cosine + first_half * sine_part], axis=-1)

def span_layout(lengths, prefix, prefill, page_size):
    request_end = jnp.cumsum(lengths).astype(jnp.int32)
    request_start = request_end - lengths
    token_index = jnp.arange(prefill, dtype=jnp.int32)
    request = lax.optimization_barrier(jnp.sum((token_index[:, None] >= request_end[None, :]).astype(jnp.int32), axis=1))
    onehot = (request[:, None] == jnp.arange(lengths.shape[0], dtype=jnp.int32)[None, :]).astype(jnp.int32)
    token_start = lax.optimization_barrier(jnp.sum(onehot * request_start[None, :], axis=1))
    token_prefix = lax.optimization_barrier(jnp.sum(onehot * prefix[None, :], axis=1))
    return (request, token_prefix * page_size + token_index - token_start)

def prefix_keys(prefix, pages, page_size):
    slot_count = prefix.shape[0] * pages * page_size
    key_index = jnp.arange(slot_count, dtype=jnp.int32)
    key_owner = key_index // (pages * page_size)
    within = key_index // page_size % pages
    onehot = (key_owner[:, None] == jnp.arange(prefix.shape[0], dtype=jnp.int32)[None, :]).astype(jnp.int32)
    page_limit = lax.optimization_barrier(jnp.sum(onehot * prefix[None, :], axis=1))
    return (key_owner, within < page_limit)

def product(form, left, right):
    return jnp.einsum(form, left.astype(jnp.float32), right.astype(jnp.float32))

def attend(query_rows, new_keys, new_vals, pre_keys, pre_vals, cache_keys, cache_vals, request, key_owner, usable, filled):
    prefill = request.shape[0]
    factor = 1.0 / math.sqrt(query_rows.shape[-1])
    head_q = query_rows[:prefill]
    score_prefix = product('qhd,md->qhm', head_q, pre_keys) * factor
    score_span = product('qhd,kd->qhk', head_q, new_keys[:prefill]) * factor
    token_index = jnp.arange(prefill, dtype=jnp.int32)
    mask_prefix = ((request[:, None] == key_owner[None, :]) & usable[None, :])[:, None, :]
    mask_span = ((request[:, None] == request[None, :]) & (token_index[None, :] <= token_index[:, None]))[:, None, :]
    score_prefix = jnp.where(mask_prefix, score_prefix, NEGATIVE)
    score_span = jnp.where(mask_span, score_span, NEGATIVE)
    peak_score = jnp.maximum(lax.optimization_barrier(jnp.max(score_prefix, axis=-1, keepdims=True)), lax.optimization_barrier(jnp.max(score_span, axis=-1, keepdims=True)))
    exp_prefix = jnp.where(mask_prefix, jnp.exp(score_prefix - peak_score), 0.0)
    exp_span = jnp.where(mask_span, jnp.exp(score_span - peak_score), 0.0)
    denominator = lax.optimization_barrier(jnp.sum(exp_prefix, axis=-1, keepdims=True)) + lax.optimization_barrier(jnp.sum(exp_span, axis=-1, keepdims=True))
    weight_prefix = (exp_prefix / denominator).astype(jnp.bfloat16)
    weight_span = (exp_span / denominator).astype(jnp.bfloat16)
    context_pre = product('qhm,md->qhd', weight_prefix, pre_vals) + product('qhk,kd->qhd', weight_span, new_vals[:prefill])
    head_d = query_rows[prefill:]
    score_cache = product('dhx,dtx->dht', head_d, cache_keys) * factor
    score_own = product('dhx,dx->dh', head_d, new_keys[prefill:])[..., None] * factor
    mask_cache = (jnp.arange(cache_keys.shape[1], dtype=jnp.int32)[None, :] < filled[:, None])[:, None, :]
    score_cache = jnp.where(mask_cache, score_cache, NEGATIVE)
    peak_dec = jnp.maximum(lax.optimization_barrier(jnp.max(score_cache, axis=-1, keepdims=True)), score_own)
    exp_cache = jnp.where(mask_cache, jnp.exp(score_cache - peak_dec), 0.0)
    exp_own = jnp.exp(score_own - peak_dec)
    denom_dec = lax.optimization_barrier(jnp.sum(exp_cache, axis=-1, keepdims=True)) + exp_own
    weight_cache = (exp_cache / denom_dec).astype(jnp.bfloat16)
    weight_own = (exp_own / denom_dec).astype(jnp.bfloat16)
    context_dec = product('dht,dtx->dhx', weight_cache, cache_vals) + weight_own.astype(jnp.float32) * new_vals[prefill:][:, None, :].astype(jnp.float32)
    return jnp.concatenate([context_pre, context_dec], axis=0).astype(jnp.bfloat16)

def reference(inputs, entry_gain, exit_gain, query_weight, key_value_matrix, output_weight, page_pool, page_table, positions, request_lengths, prefix_pages, source_pages, target_pages):
    decode_row_count = PRE + DECODE_ROWS
    query_group_width = QUERY_HEADS // KEY_VALUE_HEADS
    hidden_parts = []
    normed_parts = []
    for replica in range(N_REPLICA):
        peer = (replica + 1) % N_REPLICA
        stream = inputs[replica * decode_row_count:(replica + 1) * decode_row_count]
        own_pool = page_pool[replica * REPLICA_PAGES:(replica + 1) * REPLICA_PAGES]
        peer_pool = page_pool[peer * REPLICA_PAGES:(peer + 1) * REPLICA_PAGES]
        row_page_list = page_table[replica * DECODE_ROWS:(replica + 1) * DECODE_ROWS]
        dec_positions = positions[replica * DECODE_ROWS:(replica + 1) * DECODE_ROWS]
        req_lengths = request_lengths[replica]
        prefix_count = prefix_pages[replica]
        source = source_pages[replica]
        destination = target_pages[replica]
        normed = norm_rows(stream.astype(jnp.float32), entry_gain).astype(jnp.bfloat16)
        request, span_pos = span_layout(req_lengths, prefix_count, PRE, PAGE_TOKENS)
        all_pos = jnp.concatenate([span_pos, dec_positions])
        query_rows = jnp.dot(normed, query_weight, preferred_element_type=jnp.float32).reshape(decode_row_count, QUERY_HEADS, HEAD_SIZE)
        query_rows = rotate(query_rows, all_pos).astype(jnp.bfloat16)
        key_value_pairs = jnp.dot(normed, key_value_matrix, preferred_element_type=jnp.float32).astype(jnp.bfloat16)
        key_value_pairs = key_value_pairs.reshape(decode_row_count, KEY_VALUE_HEADS, 2, HEAD_SIZE)
        new_keys = rotate(key_value_pairs[:, :, 0].astype(jnp.float32), all_pos).astype(jnp.bfloat16)
        new_vals = key_value_pairs[:, :, 1]
        moved_requests = peer_pool[source.reshape(-1)]
        valid = (jnp.arange(PREFIX_PAGE_MAX, dtype=jnp.int32)[None, :] < prefix_count[:, None]).reshape(-1)
        target = jnp.where(valid, destination.reshape(-1), REPLICA_PAGES).astype(jnp.int32)
        updated_page_store = own_pool.at[target].set(moved_requests, mode='drop')
        prefill_cache = moved_requests.reshape(MOVED_REQUESTS * PREFIX_PAGE_MAX * PAGE_TOKENS, KEY_VALUE_HEADS, 2, HEAD_SIZE)
        decode_cache = updated_page_store[row_page_list].reshape(DECODE_ROWS, TABLE_PAGES * PAGE_TOKENS, KEY_VALUE_HEADS, 2, HEAD_SIZE)
        key_owner, usable = prefix_keys(prefix_count, PREFIX_PAGE_MAX, PAGE_TOKENS)
        grouped_queries = query_rows.reshape(decode_row_count, KEY_VALUE_HEADS, query_group_width, HEAD_SIZE)
        context = jax.vmap(attend, in_axes=(1, 1, 1, 1, 1, 2, 2, None, None, None, None), out_axes=1)(grouped_queries, new_keys, new_vals, prefill_cache[:, :, 0], prefill_cache[:, :, 1], decode_cache[:, :, :, 0], decode_cache[:, :, :, 1], request, key_owner, usable, dec_positions)
        context = context.reshape(decode_row_count, QUERY_HEADS * HEAD_SIZE)
        mixed_sum = stream.astype(jnp.float32) + jnp.dot(context, output_weight, preferred_element_type=jnp.float32)
        hidden_parts.append(mixed_sum.astype(jnp.bfloat16))
        normed_parts.append(norm_rows(mixed_sum, exit_gain).astype(jnp.bfloat16))
    return (jnp.concatenate(hidden_parts, axis=0), jnp.concatenate(normed_parts, axis=0))
```

```python
import functools
import math

import jax
import jax.numpy as jnp
import numpy as np
from jax import lax
from jax.experimental import pallas as pl
from jax.experimental.pallas import tpu as pltpu
from jax.sharding import PartitionSpec as P

QUERY_HEADS = 64
KEY_VALUE_HEADS = 8
HEAD_SIZE = 128
EPS = 1e-06
THETA = 1000000.0
NEGATIVE = -1e30
FACTOR = 1.0 / math.sqrt(HEAD_SIZE)

ORDER = (0, 2, 4, 6, 7, 5, 3, 1)
RING = len(ORDER)
PLACE = tuple(ORDER.index(t) for t in range(RING))
FORWARD = [(ORDER[i], ORDER[(i + 1) % RING]) for i in range(RING)]
BACKWARD = [(b, a) for a, b in FORWARD]

VMEM = pltpu.CompilerParams(vmem_limit_bytes=48 * 1024 * 1024)


def dot(left, right):
    return jnp.dot(left, right, preferred_element_type=jnp.float32)


def dot_t(left, right):
    return lax.dot_general(
        left, right, (((1,), (1,)), ((), ())), preferred_element_type=jnp.float32
    )


def turned(values, cosine, sine):
    return values * cosine + pltpu.roll(values, HEAD_SIZE // 2, 1) * sine


def span_layout(lengths, prefix, prefill, page_size):
    request_end = jnp.cumsum(lengths)
    request_start = request_end - lengths
    token_index = jnp.arange(prefill, dtype=jnp.int32)
    request = jnp.sum((token_index[:, None] >= request_end[None, :]).astype(jnp.int32), axis=1)
    onehot = (request[:, None] == jnp.arange(lengths.shape[0], dtype=jnp.int32)[None, :]).astype(
        jnp.int32
    )
    token_start = jnp.sum(onehot * request_start[None, :], axis=1)
    token_prefix = jnp.sum(onehot * prefix[None, :], axis=1)
    return (request, token_prefix * page_size + token_index - token_start)


def tables(positions):
    half_dim = HEAD_SIZE // 2
    frequency = jnp.exp(
        jnp.arange(half_dim, dtype=jnp.float32) * (-2.0 * math.log(THETA) / HEAD_SIZE)
    )
    angles = positions.astype(jnp.float32)[:, None] * frequency[None, :]
    cosine, sine = jnp.cos(angles), jnp.sin(angles)
    return (
        jnp.concatenate([cosine, cosine], axis=1),
        jnp.concatenate([-sine, sine], axis=1),
    )


def pairs_kernel(blocks, x_ref, gain_ref, w_ref, out_ref):
    scaled = (x_ref[...].astype(jnp.float32) * gain_ref[...].astype(jnp.float32)).astype(
        jnp.bfloat16
    )
    out_ref[0] = dot(scaled, w_ref[...])


def pairs_partial(x, gain_row, matrix, blocks, me):
    rows, width = x.shape
    columns = matrix.shape[1] // RING
    return pl.pallas_call(
        pairs_kernel,
        grid_spec=pltpu.PrefetchScalarGridSpec(
            num_scalar_prefetch=1,
            grid=(RING,),
            in_specs=[
                pl.BlockSpec((rows, width), lambda k, b: (0, 0)),
                pl.BlockSpec((1, width), lambda k, b: (0, b[0])),
                pl.BlockSpec((width, columns), lambda k, b: (0, b[k])),
            ],
            out_specs=pl.BlockSpec((1, rows, columns), lambda k, b: (k, 0, 0)),
        ),
        out_shape=jax.ShapeDtypeStruct((RING, rows, columns), jnp.float32),
        compiler_params=VMEM,
        name="pairs_partial",
    )(blocks, x, gain_row, matrix)


def add_kernel(arrived_ref, part_ref, out_ref):
    out_ref[...] = (arrived_ref[...].astype(jnp.float32) + part_ref[0]).astype(out_ref.dtype)


def add_part(arrived, parts, k, half, dtype=jnp.bfloat16):
    rows, columns = arrived.shape
    return pl.pallas_call(
        add_kernel,
        grid=(1,),
        in_specs=[
            pl.BlockSpec((rows, columns), lambda i: (0, 0)),
            pl.BlockSpec((1, rows, columns), lambda i: (k, half, 0)),
        ],
        out_specs=pl.BlockSpec((rows, columns), lambda i: (0, 0)),
        out_shape=jax.ShapeDtypeStruct((rows, columns), dtype),
        compiler_params=VMEM,
        name="add_part",
    )(arrived, parts)


def last_kernel(arrived_ref, part_ref, x_ref, mixed_ref, hidden_ref, square_ref):
    mixed = x_ref[...].astype(jnp.float32) + (arrived_ref[...].astype(jnp.float32) + part_ref[0])
    mixed_ref[...] = mixed
    hidden_ref[...] = mixed.astype(jnp.bfloat16)
    square_ref[...] = jnp.sum(mixed * mixed, axis=1, keepdims=True)


def last_part(arrived, parts, half, x):
    rows, columns = arrived.shape
    flat = pl.BlockSpec((rows, columns), lambda i: (0, 0))
    return pl.pallas_call(
        last_kernel,
        grid=(1,),
        in_specs=[flat, pl.BlockSpec((1, rows, columns), lambda i: (0, half, 0)), flat],
        out_specs=[flat, flat, pl.BlockSpec((rows, 1), lambda i: (0, 0))],
        out_shape=[
            jax.ShapeDtypeStruct((rows, columns), jnp.float32),
            jax.ShapeDtypeStruct((rows, columns), jnp.bfloat16),
            jax.ShapeDtypeStruct((rows, 1), jnp.float32),
        ],
        compiler_params=VMEM,
        name="last_part",
    )(arrived, parts, x)


def query_kernel(width, blocks, *refs):
    pieces, (gain_ref, w_ref, cos_ref, sin_ref) = refs[: 2 * RING], refs[2 * RING : 2 * RING + 4]
    q_ref, inv_ref, scaled, total, squares = refs[2 * RING + 4 :]
    step = pl.program_id(0)
    half = pieces[0].shape[0]
    gain = gain_ref[...].astype(jnp.float32)

    @pl.when(step == 0)
    def _():
        total[...] = jnp.zeros_like(total)
        squares[...] = jnp.zeros_like(squares)

    for k in range(RING):

        @pl.when(step == k)
        def _(k=k):
            for side, piece in enumerate((pieces[(RING - k) % RING], pieces[RING + k])):
                rows = slice(side * half, (side + 1) * half)
                values = piece[...].astype(jnp.float32)
                squares[rows] += jnp.sum(values * values, axis=1, keepdims=True)
                scaled[rows] = (values * gain).astype(jnp.bfloat16)

    total[...] += dot(scaled[...], w_ref[...])

    @pl.when(step == RING - 1)
    def _():
        inv = lax.rsqrt(squares[...] / width + EPS)
        inv_ref[...] = inv
        for head in range(q_ref.shape[1] // HEAD_SIZE):
            at = slice(head * HEAD_SIZE, (head + 1) * HEAD_SIZE)
            q_ref[:, at] = turned(total[:, at] * inv, cos_ref[...], sin_ref[...]).astype(
                jnp.bfloat16
            )


def query_rows(forward, backward, gain_row, weight, cosine, sine, blocks):
    half, depth = forward[0].shape
    rows, width = 2 * half, weight.shape[1]
    whole = pl.BlockSpec((half, depth), lambda k, b: (0, 0), pipeline_mode=pl.Buffered(1))
    table = pl.BlockSpec((rows, HEAD_SIZE), lambda k, b: (0, 0))
    return pl.pallas_call(
        functools.partial(query_kernel, weight.shape[0]),
        grid_spec=pltpu.PrefetchScalarGridSpec(
            num_scalar_prefetch=1,
            grid=(RING,),
            in_specs=[whole] * (2 * RING)
            + [
                pl.BlockSpec((1, depth), lambda k, b: (0, b[k])),
                pl.BlockSpec((depth, width), lambda k, b: (b[k], 0)),
                table,
                table,
            ],
            out_specs=[
                pl.BlockSpec((rows, width), lambda k, b: (0, 0)),
                pl.BlockSpec((rows, 1), lambda k, b: (0, 0)),
            ],
            scratch_shapes=[
                pltpu.VMEM((rows, depth), jnp.bfloat16),
                pltpu.VMEM((rows, width), jnp.float32),
                pltpu.VMEM((rows, 1), jnp.float32),
            ],
        ),
        out_shape=[
            jax.ShapeDtypeStruct((rows, width), jnp.bfloat16),
            jax.ShapeDtypeStruct((rows, 1), jnp.float32),
        ],
        compiler_params=VMEM,
        name="query_rows",
    )(blocks, *forward, *backward, gain_row, weight, cosine, sine)


def new_pairs(pairs_ref, inv_ref, cos_ref, sin_ref):
    pairs = (pairs_ref[...] * inv_ref[...]).astype(jnp.bfloat16)
    keys = turned(pairs[:, :HEAD_SIZE].astype(jnp.float32), cos_ref[...], sin_ref[...])
    return keys.astype(jnp.bfloat16), pairs[:, HEAD_SIZE:]


def decode_kernel(
    page_size, q_ref, cache_ref, pairs_ref, inv_ref, cos_ref, sin_ref, page_ref, pos_ref,
    out_ref, count, new_key, new_value,
):
    @pl.when(pl.program_id(0) == 0)
    def _():
        token = lax.broadcasted_iota(jnp.int32, count.shape, 1)
        page, offset = token // page_size, token % page_size
        times = jnp.zeros(count.shape, jnp.float32)
        for j in range(page_ref.shape[1]):
            hit = (page == page_ref[:, j : j + 1]) & (offset + j * page_size < pos_ref[...])
            times += jnp.where(hit, 1.0, 0.0)
        count[...] = times
        keys, values = new_pairs(pairs_ref, inv_ref, cos_ref, sin_ref)
        new_key[...] = keys.astype(jnp.float32)
        new_value[...] = values.astype(jnp.float32)

    q = q_ref[...]
    times = count[...]
    score = jnp.where(times > 0, dot_t(q, cache_ref[:, :HEAD_SIZE]) * FACTOR, NEGATIVE)
    own = jnp.sum(q.astype(jnp.float32) * new_key[...], axis=1, keepdims=True) * FACTOR
    peak = jnp.maximum(jnp.max(score, axis=1, keepdims=True), own)
    grown, grown_own = jnp.exp(score - peak), jnp.exp(own - peak)
    scale = 1.0 / (jnp.sum(grown * times, axis=1, keepdims=True) + grown_own)
    weight = (grown * scale).astype(jnp.bfloat16).astype(jnp.float32) * times
    weight_own = (grown_own * scale).astype(jnp.bfloat16).astype(jnp.float32)
    context = dot(weight.astype(jnp.bfloat16), cache_ref[:, HEAD_SIZE:])
    out_ref[...] = (context + weight_own * new_value[...]).astype(jnp.bfloat16)


def decode_context(q, cache, pairs, inv, cosine, sine, page_table, positions, page_size):
    rows, width = q.shape
    tokens = cache.shape[0]
    whole = lambda array: pl.BlockSpec(array.shape, lambda h: (0, 0))
    head = pl.BlockSpec((rows, HEAD_SIZE), lambda h: (0, h))
    return pl.pallas_call(
        functools.partial(decode_kernel, page_size),
        grid=(width // HEAD_SIZE,),
        in_specs=[head]
        + [whole(a) for a in (cache, pairs, inv, cosine, sine, page_table, positions)],
        out_specs=head,
        scratch_shapes=[
            pltpu.VMEM((rows, tokens), jnp.float32),
            pltpu.VMEM((rows, HEAD_SIZE), jnp.float32),
            pltpu.VMEM((rows, HEAD_SIZE), jnp.float32),
        ],
        out_shape=jax.ShapeDtypeStruct((rows, width), jnp.bfloat16),
        compiler_params=VMEM,
        name="decode_context",
    )(q, cache, pairs, inv, cosine, sine, page_table, positions)


def prefill_kernel(
    q_ref, prefix_ref, pairs_ref, inv_ref, cos_ref, sin_ref, request_ref, column_ref, owner_ref,
    out_ref, bias, keys, values,
):
    old = prefix_ref.shape[0]

    @pl.when(pl.program_id(0) == 0)
    def _():
        rows = request_ref.shape[0]
        request = request_ref[...]
        bias[:, :old] = jnp.where(request == owner_ref[...], 0.0, NEGATIVE)
        row = lax.broadcasted_iota(jnp.int32, (rows, rows), 0)
        column = lax.broadcasted_iota(jnp.int32, (rows, rows), 1)
        allowed = (request == column_ref[...]) & (column <= row)
        bias[:, old:] = jnp.where(allowed, 0.0, NEGATIVE)
        new_keys, new_values = new_pairs(pairs_ref, inv_ref, cos_ref, sin_ref)
        keys[:old] = prefix_ref[:, :HEAD_SIZE]
        keys[old:] = new_keys
        values[:old] = prefix_ref[:, HEAD_SIZE:]
        values[old:] = new_values

    score = dot_t(q_ref[...], keys[...]) * FACTOR + bias[...]
    grown = jnp.exp(score - jnp.max(score, axis=1, keepdims=True))
    scale = 1.0 / jnp.sum(grown, axis=1, keepdims=True)
    weight = (grown * scale).astype(jnp.bfloat16)
    out_ref[...] = dot(weight, values[...]).astype(jnp.bfloat16)


def prefill_context(q, prefix, pairs, inv, cosine, sine, request, owner):
    rows, width = q.shape
    tokens = prefix.shape[0] + rows
    operands = (prefix, pairs, inv, cosine, sine, request[:, None], request[None, :], owner[None, :])
    head = pl.BlockSpec((rows, HEAD_SIZE), lambda h: (0, h))
    return pl.pallas_call(
        prefill_kernel,
        grid=(width // HEAD_SIZE,),
        in_specs=[head] + [pl.BlockSpec(a.shape, lambda h: (0, 0)) for a in operands],
        out_specs=head,
        scratch_shapes=[
            pltpu.VMEM((rows, tokens), jnp.float32),
            pltpu.VMEM((tokens, HEAD_SIZE), jnp.bfloat16),
            pltpu.VMEM((tokens, HEAD_SIZE), jnp.bfloat16),
        ],
        out_shape=jax.ShapeDtypeStruct((rows, width), jnp.bfloat16),
        compiler_params=VMEM,
        name="prefill_context",
    )(q, *operands)


def output_kernel(blocks, context_ref, w_ref, out_ref):
    out_ref[0] = dot(context_ref[...], w_ref[...])


def output_partial(context, weight, blocks):
    rows, depth = context.shape
    columns = weight.shape[1] // RING
    return pl.pallas_call(
        output_kernel,
        grid_spec=pltpu.PrefetchScalarGridSpec(
            num_scalar_prefetch=1,
            grid=(RING,),
            in_specs=[
                pl.BlockSpec((rows, depth), lambda k, b: (0, 0)),
                pl.BlockSpec((depth, columns), lambda k, b: (0, b[k])),
            ],
            out_specs=pl.BlockSpec((1, rows, columns), lambda k, b: (k, 0, 0)),
        ),
        out_shape=jax.ShapeDtypeStruct((RING, rows, columns), jnp.float32),
        compiler_params=VMEM,
        name="output_partial",
    )(blocks, context, weight)


def gather_ring(piece, route):
    pieces = [piece]
    for _ in range(RING - 1):
        pieces.append(lax.ppermute(pieces[-1], "tensor", route))
    return pieces


def first_part(parts, k, half, rows):
    return parts[k, half * rows : (half + 1) * rows].astype(jnp.bfloat16)


def scatter_ring(parts, half, rows, last):
    route = BACKWARD if half else FORWARD
    places = range(1, RING) if half else range(RING - 1, 0, -1)
    running = None
    for k in places:
        if running is None:
            running = first_part(parts, k, half, rows)
        else:
            running = add_part(running, parts, k, half)
        running = lax.ppermute(running, "tensor", route)
    return last(running)


def sum_squares(squares):
    for low in (1, 2, 4):
        squares = squares + lax.ppermute(
            squares, "tensor", [(t, t ^ low) for t in range(RING)]
        )
    return squares


def body(
    inputs,
    entry_gain,
    exit_gain,
    query_weight,
    key_value_matrix,
    output_weight,
    page_pool,
    page_table,
    positions,
    request_lengths,
    prefix_pages,
    source_pages,
    target_pages,
):
    decode = page_table.shape[0]
    prefill = inputs.shape[0] - decode
    page_count, page_size, _ = page_pool.shape
    me = lax.axis_index("tensor")
    width = inputs.shape[1]
    per_device = query_weight.shape[1] // HEAD_SIZE
    group = me * per_device // (QUERY_HEADS // KEY_VALUE_HEADS)
    pair = 2 * HEAD_SIZE

    own_pool = lax.dynamic_slice_in_dim(page_pool, group * pair, pair, 2)
    peer_pool = lax.ppermute(own_pool, "replica", [(0, 1), (1, 0)])
    prefix = prefix_pages[0]
    page_max = target_pages.shape[2]
    arrived = peer_pool[source_pages.reshape(-1)]
    usable = jnp.arange(page_max, dtype=jnp.int32)[None, :] < prefix[:, None]
    target = jnp.where(usable.reshape(-1), target_pages.reshape(-1), page_count)
    cache = own_pool.at[target].set(arrived, mode="drop").reshape(-1, pair)
    prefix_rows = arrived.reshape(-1, pair)
    slots = jnp.where(usable, jnp.arange(prefix.shape[0], dtype=jnp.int32)[:, None], -1)
    owner = jnp.repeat(slots.reshape(-1), page_size)

    request, span = span_layout(request_lengths[0], prefix, prefill, page_size)
    cosine, sine = tables(jnp.concatenate([span, positions]))
    gain_row = entry_gain[None, :]
    spans = (slice(0, prefill), slice(prefill, prefill + decode))

    def attend(which, q, pairs, inv):
        at = spans[which]
        if which == 0:
            return prefill_context(
                q, prefix_rows, pairs, inv, cosine[at], sine[at], request, owner
            )
        return decode_context(
            q, cache, pairs, inv, cosine[at], sine[at], page_table, positions[:, None], page_size
        )

    exit_row = lax.dynamic_slice_in_dim(exit_gain, me * width, width, 0).astype(jnp.float32)

    def normed(mixed, squares):
        inv = lax.rsqrt(squares / exit_gain.shape[0] + EPS)
        return (mixed * inv * exit_row[None, :]).astype(jnp.bfloat16)

    if lax.axis_size("tensor") == RING:
        blocks = jnp.asarray(ORDER, jnp.int32)[
            (jnp.asarray(PLACE, jnp.int32)[me] + jnp.arange(RING)) % RING
        ]
        parts = pairs_partial(inputs, gain_row, key_value_matrix, blocks, me)
        pairs = [
            scatter_ring(
                parts, which, prefill, lambda r, w=which: add_part(r, parts, 0, w, jnp.float32)
            )
            for which in (0, 1)
        ]
        half = prefill // 2
        hidden, out = [None, None], [None, None]
        for which in (1, 0):
            low = spans[which].start
            ahead, back = inputs[low : low + half], inputs[low + half : low + 2 * half]
            at = spans[which]
            q, inv = query_rows(
                gather_ring(ahead, FORWARD), gather_ring(back, BACKWARD),
                gain_row, query_weight, cosine[at], sine[at], blocks,
            )
            context = attend(which, q, pairs[which], inv)
            partial = output_partial(context, output_weight, blocks)
            sides = [
                scatter_ring(
                    partial, side, half, lambda r, s=side, x=x: last_part(r, partial, s, x)
                )
                for side, x in enumerate((ahead, back))
            ]
            mixed, kept, squares = [jnp.concatenate(both, axis=0) for both in zip(*sides)]
            hidden[which] = kept
            out[which] = normed(mixed, sum_squares(squares[:, 0])[:, None])
        return jnp.concatenate(hidden, axis=0), jnp.concatenate(out, axis=0)

    rows = lax.all_gather(inputs, "tensor", axis=1, tiled=True).astype(jnp.float32)
    inv = lax.rsqrt(jnp.mean(rows * rows, axis=1, keepdims=True) + EPS)
    scaled = (rows * inv * entry_gain.astype(jnp.float32)).astype(jnp.bfloat16)
    own = lax.dynamic_slice_in_dim(scaled, me * width, width, 1)
    pairs = lax.psum(dot(own, key_value_matrix), "tensor")
    pairs = lax.dynamic_slice_in_dim(pairs, group * pair, pair, 1)
    q = dot(scaled, query_weight).reshape(-1, per_device, HEAD_SIZE)
    swapped = jnp.roll(q, HEAD_SIZE // 2, 2)
    q = (q * cosine[:, None] + swapped * sine[:, None]).astype(jnp.bfloat16)
    q = q.reshape(-1, per_device * HEAD_SIZE)
    one = jnp.ones_like(inv)
    context = jnp.concatenate([attend(w, q[spans[w]], pairs[spans[w]], one[spans[w]]) for w in (0, 1)])
    summed = lax.psum_scatter(
        dot(context, output_weight), "tensor", scatter_dimension=1, tiled=True
    )
    mixed = inputs.astype(jnp.float32) + summed
    squares = lax.psum(jnp.sum(mixed * mixed, axis=1), "tensor")[:, None]
    return mixed.astype(jnp.bfloat16), normed(mixed, squares)


def solution(mesh):
    rows = ("groups", "replica")
    return jax.shard_map(
        body,
        mesh=mesh,
        in_specs=(
            P(rows, "tensor"),
            P(),
            P(),
            P(None, "tensor"),
            P("tensor", None),
            P("tensor", None),
            P(rows, None, None),
            P(rows, None),
            P(rows),
            P(rows, None),
            P(rows, None),
            P(rows, None, None),
            P(rows, None, None),
        ),
        out_specs=(P(rows, "tensor"), P(rows, "tensor")),
        check_vma=False,
    )
```

```python
import functools
import math

import jax
import jax.numpy as jnp
import numpy as np
from jax import lax
from jax.experimental import pallas as pl
from jax.experimental.pallas import tpu as pltpu
from jax.sharding import PartitionSpec as P

QUERY_HEADS = 64
KEY_VALUE_HEADS = 8
HEAD_SIZE = 128
EPS = 1e-06
THETA = 1000000.0
NEGATIVE = -1e30
FACTOR2 = math.log2(math.e) / math.sqrt(HEAD_SIZE)

ORDER = (0, 2, 4, 6, 7, 5, 3, 1)
RING = len(ORDER)
FORWARD = [(ORDER[i], ORDER[(i + 1) % RING]) for i in range(RING)]
BACKWARD = [(b, a) for a, b in FORWARD]

VMEM = pltpu.CompilerParams(vmem_limit_bytes=48 * 1024 * 1024)


def dot(left, right):
    return jnp.dot(left, right, preferred_element_type=jnp.float32)


def dot_t(left, right):
    return lax.dot_general(
        left, right, (((1,), (1,)), ((), ())), preferred_element_type=jnp.float32
    )


def turned(values, cosine, sine):
    return values * cosine + pltpu.roll(values, HEAD_SIZE // 2, 1) * sine


def span_layout(lengths, prefix, prefill, page_size):
    request_end = jnp.cumsum(lengths)
    request_start = request_end - lengths
    token_index = jnp.arange(prefill, dtype=jnp.int32)
    request = jnp.sum((token_index[:, None] >= request_end[None, :]).astype(jnp.int32), axis=1)
    onehot = (request[:, None] == jnp.arange(lengths.shape[0], dtype=jnp.int32)[None, :]).astype(
        jnp.int32
    )
    token_start = jnp.sum(onehot * request_start[None, :], axis=1)
    token_prefix = jnp.sum(onehot * prefix[None, :], axis=1)
    return (request, token_prefix * page_size + token_index - token_start)


def tables(positions):
    half_dim = HEAD_SIZE // 2
    frequency = jnp.exp(
        jnp.arange(half_dim, dtype=jnp.float32) * (-2.0 * math.log(THETA) / HEAD_SIZE)
    )
    angles = positions.astype(jnp.float32)[:, None] * frequency[None, :]
    cosine, sine = jnp.cos(angles), jnp.sin(angles)
    return (
        jnp.concatenate([cosine, cosine], axis=1),
        jnp.concatenate([-sine, sine], axis=1),
    )


def cost(flops, moved, transcendentals=0):
    return pl.CostEstimate(flops=flops, bytes_accessed=moved, transcendentals=transcendentals)


def shaped(shape, dtype):
    return jax.ShapeDtypeStruct(shape, dtype)


def pairs_kernel(blocks, x_ref, gain_ref, w_ref, out_ref, forward_ref, backward_ref, scaled):
    k = pl.program_id(0)

    @pl.when(k == 0)
    def _():
        gain = gain_ref[...].astype(jnp.float32)
        scaled[...] = (x_ref[...].astype(jnp.float32) * gain).astype(jnp.bfloat16)

    result = dot(scaled[...], w_ref[...]).astype(jnp.bfloat16)
    out_ref[0] = result
    half = forward_ref.shape[0]

    @pl.when(k == RING - 1)
    def _():
        forward_ref[...] = result[:half]

    @pl.when(k == 1)
    def _():
        backward_ref[...] = result[half:]


def pairs_partial(x, gain_row, matrix, blocks):
    rows, width = x.shape
    columns = matrix.shape[1] // RING
    first = pl.BlockSpec((rows // 2, columns), lambda k, b: (0, 0))
    return pl.pallas_call(
        pairs_kernel,
        grid_spec=pltpu.PrefetchScalarGridSpec(
            num_scalar_prefetch=1,
            grid=(RING,),
            in_specs=[
                pl.BlockSpec((rows, width), lambda k, b: (0, 0)),
                pl.BlockSpec((1, width), lambda k, b: (0, b[0])),
                pl.BlockSpec((width, columns), lambda k, b: (0, b[k])),
            ],
            out_specs=[pl.BlockSpec((1, rows, columns), lambda k, b: (k, 0, 0)), first, first],
            scratch_shapes=[pltpu.VMEM((rows, width), jnp.bfloat16)],
        ),
        out_shape=[
            shaped((RING, rows, columns), jnp.bfloat16),
            shaped((rows // 2, columns), jnp.bfloat16),
            shaped((rows // 2, columns), jnp.bfloat16),
        ],
        compiler_params=VMEM,
        cost_estimate=cost(2 * x.size * matrix.shape[1], 2 * (x.size + 2 * matrix.size)),
        name="pairs_partial",
    )(blocks, x, gain_row, matrix)


def add_pairs_kernel(a_ref, b_ref, pa_ref, pb_ref, oa_ref, ob_ref):
    for arrived, part, out in ((a_ref, pa_ref, oa_ref), (b_ref, pb_ref, ob_ref)):
        out[...] = (arrived[...].astype(jnp.float32) + part[0].astype(jnp.float32)).astype(
            out.dtype
        )


def add_pairs(ahead, back, parts, ka, kb, dtype):
    rows, columns = ahead.shape
    flat = pl.BlockSpec((rows, columns), lambda i: (0, 0))
    return pl.pallas_call(
        add_pairs_kernel,
        grid=(1,),
        in_specs=[
            flat,
            flat,
            pl.BlockSpec((1, rows, columns), lambda i: (ka, 0, 0)),
            pl.BlockSpec((1, rows, columns), lambda i: (kb, 1, 0)),
        ],
        out_specs=[flat, flat],
        out_shape=[shaped((rows, columns), dtype)] * 2,
        compiler_params=VMEM,
        cost_estimate=cost(2 * ahead.size, 16 * ahead.size),
        name="add_pairs",
    )(ahead, back, parts, parts)


def add_kernel(a_ref, b_ref, pa_ref, pb_ref, oa_ref, ob_ref):
    for arrived, part, out in ((a_ref, pa_ref, oa_ref), (b_ref, pb_ref, ob_ref)):
        out[...] = (arrived[...].astype(jnp.float32) + part[...].astype(jnp.float32)).astype(
            out.dtype
        )


def add_parts(ahead, back, part_ahead, part_back):
    rows, columns = ahead.shape
    flat = pl.BlockSpec((rows, columns), lambda i: (0, 0))
    return pl.pallas_call(
        add_kernel,
        grid=(1,),
        in_specs=[flat] * 4,
        out_specs=[flat, flat],
        out_shape=[shaped((rows, columns), ahead.dtype)] * 2,
        compiler_params=VMEM,
        cost_estimate=cost(2 * ahead.size, 16 * ahead.size),
        name="add_parts",
    )(ahead, back, part_ahead, part_back)


def last_kernel(x_ref, *refs):
    arrived, parts, (mixed_ref, hidden_ref, square_ref) = refs[:4], refs[4:8], refs[8:]
    rows = arrived[0].shape[0]
    sums = []
    for i in range(4):
        at = slice(i * rows, (i + 1) * rows)
        added = arrived[i][...].astype(jnp.float32) + parts[i][...].astype(jnp.float32)
        mixed = x_ref[at].astype(jnp.float32) + added
        mixed_ref[at] = mixed
        hidden_ref[at] = mixed.astype(jnp.bfloat16)
        sums.append(jnp.sum(mixed * mixed, axis=1, keepdims=True))
    column = jnp.broadcast_to(jnp.concatenate(sums, axis=0), (4 * rows, 128))
    square_ref[...] = column.T[: square_ref.shape[0]]


def last_parts(x, arrived, parts):
    rows, columns = x.shape
    flat = pl.BlockSpec((rows, columns), lambda i: (0, 0))
    quarter = pl.BlockSpec((rows // 4, columns), lambda i: (0, 0))
    return pl.pallas_call(
        last_kernel,
        grid=(1,),
        in_specs=[flat] + [quarter] * 8,
        out_specs=[flat, flat, pl.BlockSpec((8, rows), lambda i: (0, 0))],
        out_shape=[
            shaped((rows, columns), jnp.float32),
            shaped((rows, columns), jnp.bfloat16),
            shaped((8, rows), jnp.float32),
        ],
        compiler_params=VMEM,
        cost_estimate=cost(4 * x.size, 12 * x.size),
        name="last_parts",
    )(x, *arrived, *parts)


def norm_kernel(width, mixed_ref, square_ref, gain_ref, out_ref):
    inv = lax.rsqrt(square_ref[...].T[:, :1] / width + EPS)
    out_ref[...] = (mixed_ref[...] * inv * gain_ref[...]).astype(jnp.bfloat16)


def norm_out(mixed, squares, gain, width):
    rows, columns = mixed.shape
    return pl.pallas_call(
        functools.partial(norm_kernel, width),
        grid=(1,),
        in_specs=[pl.BlockSpec(a.shape, lambda i: (0, 0)) for a in (mixed, squares, gain)],
        out_specs=pl.BlockSpec((rows, columns), lambda i: (0, 0)),
        out_shape=shaped((rows, columns), jnp.bfloat16),
        compiler_params=VMEM,
        cost_estimate=cost(3 * mixed.size, 6 * mixed.size),
        name="norm_out",
    )(mixed, squares, gain)


def query_kernel(count, first, last, width, blocks, *refs):
    gain_ref, w_ref, *refs = refs
    if not first:
        total_in, squares_in, *refs = refs
    if last:
        cos_ref, sin_ref, *refs = refs
        *pieces, q_ref, inv_ref, scaled, total, squares = refs
    else:
        *pieces, total, squares, scaled = refs
    each = len(pieces) // count
    step = pl.program_id(0)
    rows_each = pieces[0].shape[0]
    gain = gain_ref[...].astype(jnp.float32)

    @pl.when(step == 0)
    def _():
        total[...] = jnp.zeros_like(total) if first else total_in[...]
        squares[...] = jnp.zeros_like(squares) if first else squares_in[...]

    for k in range(count):

        @pl.when(step == k)
        def _(k=k):
            for i in range(each):
                rows = slice(i * rows_each, (i + 1) * rows_each)
                values = pieces[each * k + i][...].astype(jnp.float32)
                squares[rows] += jnp.sum(values * values, axis=1, keepdims=True)
                scaled[rows] = (values * gain).astype(jnp.bfloat16)

    total[...] += dot(scaled[...], w_ref[...])

    if last:

        @pl.when(step == count - 1)
        def _():
            inv = lax.rsqrt(squares[...] / width + EPS)
            inv_ref[...] = inv
            for head in range(q_ref.shape[1] // HEAD_SIZE):
                at = slice(head * HEAD_SIZE, (head + 1) * HEAD_SIZE)
                q_ref[:, at] = turned(total[:, at] * inv, cos_ref[...], sin_ref[...]).astype(
                    jnp.bfloat16
                )


def pick(places, k, blocks):
    block = blocks[places[0]]
    for i, place in enumerate(places[1:], 1):
        block = jnp.where(k == i, blocks[place], block)
    return block


def query_part(places, pieces, gain_row, weight, blocks, sums=None, angles=None):
    count = len(places)
    rows_each, depth = pieces[0].shape
    rows, width = len(pieces) // count * rows_each, weight.shape[1]
    first, last = sums is None, angles is not None
    whole = lambda shape: pl.BlockSpec(shape, lambda k, b: (0, 0))
    sum_shapes = [(rows, width), (rows, 1)]
    in_specs = [
        pl.BlockSpec((1, depth), lambda k, b: (0, pick(places, k, b))),
        pl.BlockSpec((depth, width), lambda k, b: (pick(places, k, b), 0)),
    ]
    operands = [gain_row, weight]
    if not first:
        in_specs += [whole(s) for s in sum_shapes]
        operands += sums
    scratch = [pltpu.VMEM((rows, depth), jnp.bfloat16)]
    if last:
        in_specs += [whole((rows, HEAD_SIZE))] * 2
        operands += angles
        scratch += [pltpu.VMEM(s, jnp.float32) for s in sum_shapes]
        out_shape = [shaped((rows, width), jnp.bfloat16), shaped((rows, 1), jnp.float32)]
    else:
        out_shape = [shaped(s, jnp.float32) for s in sum_shapes]
    return pl.pallas_call(
        functools.partial(query_kernel, count, first, last, weight.shape[0]),
        grid_spec=pltpu.PrefetchScalarGridSpec(
            num_scalar_prefetch=1,
            grid=(count,),
            in_specs=in_specs + [whole((rows_each, depth))] * len(pieces),
            out_specs=[whole(s) for s in sum_shapes],
            scratch_shapes=scratch,
        ),
        out_shape=out_shape,
        compiler_params=VMEM,
        cost_estimate=cost(2 * count * rows * depth * width, count * depth * width * 4),
        name="query_part",
    )(blocks, *operands, *pieces)


def new_pairs(pairs_ref, inv_ref, cos_ref, sin_ref):
    pairs = (pairs_ref[...] * inv_ref[...]).astype(jnp.bfloat16)
    keys = turned(pairs[:, :HEAD_SIZE].astype(jnp.float32), cos_ref[...], sin_ref[...])
    return keys.astype(jnp.bfloat16), pairs[:, HEAD_SIZE:]


def decode_kernel(
    page_size, q_ref, cache_ref, pairs_ref, inv_ref, cos_ref, sin_ref, page_ref, pos_ref,
    out_ref, bias, new_key, new_value,
):
    @pl.when(pl.program_id(0) == 0)
    def _():
        token = lax.broadcasted_iota(jnp.int32, bias.shape, 1)
        page, offset = token // page_size, token % page_size
        times = jnp.zeros(bias.shape, jnp.float32)
        for j in range(page_ref.shape[1]):
            hit = (page == page_ref[:, j : j + 1]) & (offset + j * page_size < pos_ref[...])
            times += jnp.where(hit, 1.0, 0.0)
        bias[...] = jnp.where(times > 0, jnp.log2(jnp.maximum(times, 1.0)), NEGATIVE)
        keys, values = new_pairs(pairs_ref, inv_ref, cos_ref, sin_ref)
        new_key[...] = keys.astype(jnp.float32)
        new_value[...] = values.astype(jnp.float32)

    for head in range(q_ref.shape[1] // HEAD_SIZE):
        at = slice(head * HEAD_SIZE, (head + 1) * HEAD_SIZE)
        q = q_ref[:, at]
        score = dot_t(q, cache_ref[:, :HEAD_SIZE]) * FACTOR2 + bias[...]
        own = jnp.sum(q.astype(jnp.float32) * new_key[...], axis=1, keepdims=True) * FACTOR2
        peak = jnp.maximum(jnp.max(score, axis=1, keepdims=True), own)
        grown, grown_own = jnp.exp2(score - peak), jnp.exp2(own - peak)
        scale = 1.0 / (jnp.sum(grown, axis=1, keepdims=True) + grown_own)
        context = dot(grown.astype(jnp.bfloat16), cache_ref[:, HEAD_SIZE:])
        out_ref[:, at] = ((context + grown_own * new_value[...]) * scale).astype(jnp.bfloat16)


def decode_context(q, cache, pairs, inv, cosine, sine, page_table, positions, page_size):
    rows, width = positions.shape[0], q.shape[1]
    heads = min(4 * HEAD_SIZE, width)
    tokens = cache.shape[0]
    whole = lambda array: pl.BlockSpec(array.shape, lambda h: (0, 0))
    return pl.pallas_call(
        functools.partial(decode_kernel, page_size),
        grid=(width // heads,),
        in_specs=[pl.BlockSpec((rows, heads), lambda h: (0, h)), whole(cache), whole(pairs)]
        + [whole(inv), whole(cosine), whole(sine)]
        + [whole(page_table), whole(positions)],
        out_specs=pl.BlockSpec((rows, heads), lambda h: (0, h)),
        scratch_shapes=[
            pltpu.VMEM((rows, tokens), jnp.float32),
            pltpu.VMEM((rows, HEAD_SIZE), jnp.float32),
            pltpu.VMEM((rows, HEAD_SIZE), jnp.float32),
        ],
        out_shape=shaped((rows, width), jnp.bfloat16),
        compiler_params=VMEM,
        cost_estimate=cost(4 * rows * width * tokens, 8 * rows * width, 2 * width * tokens),
        name="decode_context",
    )(q, cache, pairs, inv, cosine, sine, page_table, positions)


def prefill_kernel(
    q_ref, prefix_ref, pairs_ref, inv_ref, cos_ref, sin_ref, request_ref, column_ref, owner_ref,
    out_ref, bias, keys, values,
):
    old = prefix_ref.shape[0]

    @pl.when(pl.program_id(0) == 0)
    def _():
        rows = request_ref.shape[0]
        request = request_ref[...]
        bias[:, :old] = jnp.where(request == owner_ref[...], 0.0, NEGATIVE)
        row = lax.broadcasted_iota(jnp.int32, (rows, rows), 0)
        column = lax.broadcasted_iota(jnp.int32, (rows, rows), 1)
        allowed = (request == column_ref[...]) & (column <= row)
        bias[:, old:] = jnp.where(allowed, 0.0, NEGATIVE)
        new_keys, new_values = new_pairs(pairs_ref, inv_ref, cos_ref, sin_ref)
        keys[:old] = prefix_ref[:, :HEAD_SIZE]
        keys[old:] = new_keys
        values[:old] = prefix_ref[:, HEAD_SIZE:]
        values[old:] = new_values

    for head in range(q_ref.shape[1] // HEAD_SIZE):
        at = slice(head * HEAD_SIZE, (head + 1) * HEAD_SIZE)
        score = dot_t(q_ref[:, at], keys[...]) * FACTOR2 + bias[...]
        grown = jnp.exp2(score - jnp.max(score, axis=1, keepdims=True))
        scale = 1.0 / jnp.sum(grown, axis=1, keepdims=True)
        context = dot(grown.astype(jnp.bfloat16), values[...]) * scale
        out_ref[:, at] = context.astype(jnp.bfloat16)


def prefill_context(q, prefix, pairs, inv, cosine, sine, request, owner):
    rows, width = request.shape[0], q.shape[1]
    heads = min(4 * HEAD_SIZE, width)
    tokens = prefix.shape[0] + rows
    whole = lambda array: pl.BlockSpec(array.shape, lambda h: (0, 0))
    maps = (request[:, None], request[None, :], owner[None, :])
    return pl.pallas_call(
        prefill_kernel,
        grid=(width // heads,),
        in_specs=[pl.BlockSpec((rows, heads), lambda h: (0, h)), whole(prefix), whole(pairs)]
        + [whole(inv), whole(cosine), whole(sine)]
        + [whole(a) for a in maps],
        out_specs=pl.BlockSpec((rows, heads), lambda h: (0, h)),
        scratch_shapes=[
            pltpu.VMEM((rows, tokens), jnp.float32),
            pltpu.VMEM((tokens, HEAD_SIZE), jnp.bfloat16),
            pltpu.VMEM((tokens, HEAD_SIZE), jnp.bfloat16),
        ],
        out_shape=shaped((rows, width), jnp.bfloat16),
        compiler_params=VMEM,
        cost_estimate=cost(4 * rows * width * tokens, 8 * rows * width, 2 * width * tokens),
        name="prefill_context",
    )(q, prefix, pairs, inv, cosine, sine, *maps)


def output_kernel(count, blocks, *refs):
    contexts, (wa_ref, wb_ref), outs = refs[:count], refs[count : count + 2], refs[count + 2 :]
    quarter = outs[0].shape[0]
    for w_ref, results in ((wa_ref, outs[: 2 * count]), (wb_ref, outs[2 * count :])):
        for i, context_ref in enumerate(contexts):
            result = dot(context_ref[...], w_ref[...]).astype(jnp.bfloat16)
            results[2 * i][...] = result[:quarter]
            results[2 * i + 1][...] = result[quarter:]


def output_part(contexts, weight, places, blocks, tiles=4):
    rows, depth = contexts[0].shape
    columns = weight.shape[1] // RING
    tile = columns // tiles
    count = len(contexts)
    pa, pb = places
    outs = pl.pallas_call(
        functools.partial(output_kernel, count),
        grid_spec=pltpu.PrefetchScalarGridSpec(
            num_scalar_prefetch=1,
            grid=(tiles,),
            in_specs=[pl.BlockSpec((rows, depth), lambda t, b: (0, 0))] * count
            + [
                pl.BlockSpec((depth, tile), lambda t, b: (0, b[pa] * tiles + t)),
                pl.BlockSpec((depth, tile), lambda t, b: (0, b[pb] * tiles + t)),
            ],
            out_specs=[pl.BlockSpec((rows // 2, tile), lambda t, b: (0, t))] * (4 * count),
        ),
        out_shape=[shaped((rows // 2, columns), jnp.bfloat16)] * (4 * count),
        compiler_params=VMEM,
        cost_estimate=cost(4 * count * rows * depth * columns, 8 * depth * columns),
        name="output_part",
    )(blocks, *contexts, weight, weight)
    return {pa: outs[: 2 * count], pb: outs[2 * count :]}


def after(array, *others):
    return lax.optimization_barrier((array, *others))[0]


def hop(ahead, back):
    return lax.ppermute(ahead, "tensor", FORWARD), lax.ppermute(back, "tensor", BACKWARD)


def sum_squares(squares):
    for low in (1, 2, 4):
        squares = squares + lax.ppermute(
            squares, "tensor", [(t, t ^ low) for t in range(RING)]
        )
    return squares


def body(
    inputs,
    entry_gain,
    exit_gain,
    query_weight,
    key_value_matrix,
    output_weight,
    page_pool,
    page_table,
    positions,
    request_lengths,
    prefix_pages,
    source_pages,
    target_pages,
):
    decode = page_table.shape[0]
    prefill = inputs.shape[0] - decode
    page_count, page_size, _ = page_pool.shape
    me = lax.axis_index("tensor")
    width = inputs.shape[1]
    per_device = query_weight.shape[1] // HEAD_SIZE
    group = me * per_device // (QUERY_HEADS // KEY_VALUE_HEADS)
    pair = 2 * HEAD_SIZE

    ring = lax.axis_size("tensor") == RING
    if ring:
        gathered = [[inputs[:prefill]], [inputs[prefill:]]]

        def gather_hop(*others):
            sent = [pieces[-1] for pieces in gathered]
            if others:
                sent = lax.optimization_barrier((*sent, *others))[:2]
            for pieces, arrived in zip(gathered, hop(*sent)):
                pieces.append(arrived)

        gather_hop()
        token = lax.ppermute(inputs[:16, :HEAD_SIZE], "replica", [(0, 1), (1, 0)])
        local = after(inputs, token)
        page_pool, positions, request_lengths, prefix_pages = lax.optimization_barrier(
            (page_pool, positions, request_lengths, prefix_pages, gathered[0][1])
        )[:4]

    own_pool = lax.dynamic_slice_in_dim(page_pool, group * pair, pair, 2)
    peer_pool = lax.ppermute(own_pool, "replica", [(0, 1), (1, 0)])
    prefix = prefix_pages[0]
    page_max = target_pages.shape[2]
    arrived = peer_pool[source_pages.reshape(-1)]
    usable = jnp.arange(page_max, dtype=jnp.int32)[None, :] < prefix[:, None]
    target = jnp.where(usable.reshape(-1), target_pages.reshape(-1), page_count)
    cache = own_pool.at[target].set(arrived, mode="drop").reshape(-1, pair)
    prefix_rows = arrived.reshape(-1, pair)
    slots = jnp.where(usable, jnp.arange(prefix.shape[0], dtype=jnp.int32)[:, None], -1)
    owner = jnp.repeat(slots.reshape(-1), page_size)

    request, span = span_layout(request_lengths[0], prefix, prefill, page_size)
    cosine, sine = tables(jnp.concatenate([span, positions]))
    angles = ((cosine[:prefill], sine[:prefill]), (cosine[prefill:], sine[prefill:]))
    gain_row = entry_gain[None, :]

    def attend_prefill(q, pairs, inv):
        return prefill_context(q, prefix_rows, pairs, inv, *angles[0], request, owner)

    def attend_decode(q, pairs, inv):
        return decode_context(
            q, cache, pairs, inv, *angles[1], page_table, positions[:, None], page_size
        )

    exit_row = lax.dynamic_slice_in_dim(exit_gain, me * width, width, 0)
    exit_row = exit_row.astype(jnp.float32)[None, :]

    if ring:
        place = jnp.where(me % 2 == 0, me // 2, RING - 1 - me // 2)
        places = (place + jnp.arange(RING, dtype=jnp.int32)) % RING
        blocks = jnp.where(places < RING // 2, 2 * places, 2 * (RING - places) - 1)
        parts, *moving = pairs_partial(local, gain_row, key_value_matrix, blocks)

        def pairs_hop(moving, s):
            moving = lax.optimization_barrier((*moving, gathered[0][s], gathered[1][s]))[:2]
            dtype = jnp.float32 if s == RING - 1 else jnp.bfloat16
            return add_pairs(*hop(*moving), parts, RING - 1 - s, (1 + s) % RING, dtype)

        def query(side, hops, sums=None, angles=None):
            places = [(-s if side == 0 else s) % RING for s in hops]
            pieces = [gathered[side][s] for s in hops]
            return query_part(
                places, pieces, gain_row, query_weight, blocks, sums, angles
            )

        gather_hop(*moving)
        moving = pairs_hop(moving, 1)
        gather_hop(*moving)
        moving = pairs_hop(moving, 2)
        gather_hop(*moving)
        moving = pairs_hop(moving, 3)
        sums = [query(0, (0, 1, 2, 3)), None]
        gather_hop(*moving, sums[0][1])
        moving = pairs_hop(moving, 4)
        sums[1] = query(1, (0, 1, 2, 3, 4))
        gather_hop(*moving, sums[1][1], cache, *angles[0], *angles[1])
        moving = pairs_hop(moving, 5)
        sums[0] = query(0, (4, 5), sums[0])
        gather_hop(*moving, sums[0][1])
        moving = pairs_hop(moving, 6)
        sums[1] = query(1, (5, 6), sums[1])
        sums[0] = query(0, (6,), sums[0])
        moving = lax.optimization_barrier((*moving, sums[0][1], sums[1][1]))[:2]
        pairs = pairs_hop(moving, 7)
        q, inv = query(0, (7,), sums[0], angles[0])
        prefilled = attend_prefill(q, pairs[0], inv)
        parts = [output_part([prefilled], output_weight, (7, 1), blocks), None]
        first = hop(parts[0][7][0], parts[0][1][1])
        parts[0] |= output_part([prefilled], output_weight, (6, 2), blocks)
        q, inv = query(1, (7,), sums[1], angles[1])
        second = hop(*add_parts(*first, parts[0][6][0], parts[0][2][1]))
        decoded = attend_decode(after(q, first[0]), pairs[1], inv)
        decoded_late = after(decoded, second[0])
        parts[1] = output_part([decoded_late], output_weight, (7, 1), blocks)
        parts[1] |= output_part([decoded_late], output_weight, (6, 2), blocks)
        for places in ((5, 3), (4, 0)):
            both = output_part([prefilled, decoded], output_weight, places, blocks)
            for i in range(2):
                parts[i] |= {k: both[k][2 * i : 2 * i + 2] for k in places}
        running = [second, (parts[1][7][0], parts[1][1][1])]
        for s in range(1, RING):
            for i in range(2):
                if i == 0 and s <= 2:
                    moved = second
                else:
                    moved = hop(*running[i])
                if s < RING - 1 and not (i == 0 and s == 1):
                    moved = add_parts(*moved, parts[i][RING - 1 - s][0], parts[i][1 + s][1])
                running[i] = moved
        mixed, hidden, squares = last_parts(
            inputs, [*running[0], *running[1]], [*parts[0][0], *parts[1][0]]
        )
        return hidden, norm_out(mixed, sum_squares(squares), exit_row, exit_gain.shape[0])

    rows = lax.all_gather(inputs, "tensor", axis=1, tiled=True).astype(jnp.float32)
    inv = lax.rsqrt(jnp.mean(rows * rows, axis=1, keepdims=True) + EPS)
    scaled = (rows * inv * entry_gain.astype(jnp.float32)).astype(jnp.bfloat16)
    own = lax.dynamic_slice_in_dim(scaled, me * width, width, 1)
    pairs = lax.psum(dot(own, key_value_matrix), "tensor")
    pairs = lax.dynamic_slice_in_dim(pairs, group * pair, pair, 1)
    q = dot(scaled, query_weight).reshape(-1, per_device, HEAD_SIZE)
    swapped = jnp.roll(q, HEAD_SIZE // 2, 2)
    q = (q * cosine[:, None] + swapped * sine[:, None]).astype(jnp.bfloat16)
    q = q.reshape(-1, per_device * HEAD_SIZE)
    one = jnp.ones_like(inv)
    context = [
        attend_prefill(q[:prefill], pairs[:prefill], one[:prefill]),
        attend_decode(q[prefill:], pairs[prefill:], one[prefill:]),
    ]
    context = jnp.concatenate(context, axis=0)
    summed = lax.psum_scatter(
        dot(context, output_weight), "tensor", scatter_dimension=1, tiled=True
    )
    mixed = inputs.astype(jnp.float32) + summed
    squares = lax.psum(jnp.sum(mixed * mixed, axis=1), "tensor")[:, None]
    out = mixed * lax.rsqrt(squares / exit_gain.shape[0] + EPS) * exit_row
    return mixed.astype(jnp.bfloat16), out.astype(jnp.bfloat16)


def solution(mesh):
    rows = ("groups", "replica")
    return jax.shard_map(
        body,
        mesh=mesh,
        in_specs=(
            P(rows, "tensor"),
            P(),
            P(),
            P(None, "tensor"),
            P("tensor", None),
            P("tensor", None),
            P(rows, None, None),
            P(rows, None),
            P(rows),
            P(rows, None),
            P(rows, None),
            P(rows, None, None),
            P(rows, None, None),
        ),
        out_specs=(P(rows, "tensor"), P(rows, "tensor")),
        check_vma=False,
    )
```

```python
import functools
import math

import jax
import jax.numpy as jnp
import numpy as np
from jax import lax
from jax.experimental import pallas as pl
from jax.experimental.pallas import tpu as pltpu
from jax.sharding import PartitionSpec as P

QUERY_HEADS = 64
KEY_VALUE_HEADS = 8
HEAD_SIZE = 128
EPS = 1e-06
THETA = 1000000.0
NEGATIVE = -1e30
FACTOR2 = math.log2(math.e) / math.sqrt(HEAD_SIZE)

ORDER = (0, 2, 4, 6, 7, 5, 3, 1)
RING = len(ORDER)
FAR = RING // 2
FORWARD = [(ORDER[i], ORDER[(i + 1) % RING]) for i in range(RING)]
BACKWARD = [(b, a) for a, b in FORWARD]

VMEM = pltpu.CompilerParams(vmem_limit_bytes=48 * 1024 * 1024)


def dot(left, right):
    return jnp.dot(left, right, preferred_element_type=jnp.float32)


def dot_t(left, right):
    return lax.dot_general(
        left, right, (((1,), (1,)), ((), ())), preferred_element_type=jnp.float32
    )


def turned(values, cosine, sine):
    return values * cosine + pltpu.roll(values, HEAD_SIZE // 2, 1) * sine


def span_layout(lengths, prefix, prefill, page_size):
    request_end = jnp.cumsum(lengths)
    request_start = request_end - lengths
    token_index = jnp.arange(prefill, dtype=jnp.int32)
    request = jnp.sum((token_index[:, None] >= request_end[None, :]).astype(jnp.int32), axis=1)
    onehot = (request[:, None] == jnp.arange(lengths.shape[0], dtype=jnp.int32)[None, :]).astype(
        jnp.int32
    )
    token_start = jnp.sum(onehot * request_start[None, :], axis=1)
    token_prefix = jnp.sum(onehot * prefix[None, :], axis=1)
    return (request, token_prefix * page_size + token_index - token_start)


def tables(positions):
    half_dim = HEAD_SIZE // 2
    frequency = jnp.exp(
        jnp.arange(half_dim, dtype=jnp.float32) * (-2.0 * math.log(THETA) / HEAD_SIZE)
    )
    angles = positions.astype(jnp.float32)[:, None] * frequency[None, :]
    cosine, sine = jnp.cos(angles), jnp.sin(angles)
    return (
        jnp.concatenate([cosine, cosine], axis=1),
        jnp.concatenate([-sine, sine], axis=1),
    )


def cost(flops, moved, transcendentals=0):
    return pl.CostEstimate(flops=flops, bytes_accessed=moved, transcendentals=transcendentals)


def shaped(shape, dtype):
    return jax.ShapeDtypeStruct(shape, dtype)


def pairs_kernel(blocks, x_ref, gain_ref, w_ref, out_ref, forward_ref, backward_ref, scaled):
    k = pl.program_id(0)

    @pl.when(k == 0)
    def _():
        gain = gain_ref[...].astype(jnp.float32)
        scaled[...] = (x_ref[...].astype(jnp.float32) * gain).astype(jnp.bfloat16)

    result = dot(scaled[...], w_ref[...]).astype(jnp.bfloat16)
    out_ref[0] = result
    half = forward_ref.shape[0]

    @pl.when(k == FAR)
    def _():
        forward_ref[...] = result[:half]
        backward_ref[...] = result[half:]


def pairs_partial(x, gain_row, matrix, blocks):
    rows, width = x.shape
    columns = matrix.shape[1] // RING
    first = pl.BlockSpec((rows // 2, columns), lambda k, b: (0, 0))
    return pl.pallas_call(
        pairs_kernel,
        grid_spec=pltpu.PrefetchScalarGridSpec(
            num_scalar_prefetch=1,
            grid=(RING,),
            in_specs=[
                pl.BlockSpec((rows, width), lambda k, b: (0, 0)),
                pl.BlockSpec((1, width), lambda k, b: (0, b[0])),
                pl.BlockSpec((width, columns), lambda k, b: (0, b[k])),
            ],
            out_specs=[pl.BlockSpec((1, rows, columns), lambda k, b: (k, 0, 0)), first, first],
            scratch_shapes=[pltpu.VMEM((rows, width), jnp.bfloat16)],
        ),
        out_shape=[
            shaped((RING, rows, columns), jnp.bfloat16),
            shaped((rows // 2, columns), jnp.bfloat16),
            shaped((rows // 2, columns), jnp.bfloat16),
        ],
        compiler_params=VMEM,
        cost_estimate=cost(2 * x.size * matrix.shape[1], 2 * (x.size + 2 * matrix.size)),
        name="pairs_partial",
    )(blocks, x, gain_row, matrix)


def add_pairs_kernel(a_ref, b_ref, pa_ref, pb_ref, oa_ref, ob_ref):
    rows, half = oa_ref.shape[0], oa_ref.shape[0] // 2
    sides = ((a_ref, pa_ref, oa_ref, 0), (b_ref, pb_ref, ob_ref, half))
    for arrived, part, out, low in sides:
        if arrived.shape[0] == rows:
            total = arrived[...].astype(jnp.float32) + part[0].astype(jnp.float32)
            out[...] = total.astype(out.dtype)
        else:
            out[...] = part[0]
            at = slice(low, low + half)
            total = arrived[...].astype(jnp.float32) + part[0, at].astype(jnp.float32)
            out[at] = total.astype(out.dtype)


def add_pairs(ahead, back, parts, ka, kb):
    _, rows, columns = parts.shape
    whole = lambda array: pl.BlockSpec(array.shape, lambda i: (0, 0))
    flat = pl.BlockSpec((rows, columns), lambda i: (0, 0))
    return pl.pallas_call(
        add_pairs_kernel,
        grid=(1,),
        in_specs=[
            whole(ahead),
            whole(back),
            pl.BlockSpec((1, rows, columns), lambda i: (ka, 0, 0)),
            pl.BlockSpec((1, rows, columns), lambda i: (kb, 0, 0)),
        ],
        out_specs=[flat, flat],
        out_shape=[shaped((rows, columns), jnp.bfloat16)] * 2,
        compiler_params=VMEM,
        cost_estimate=cost(2 * rows * columns, 12 * rows * columns),
        name="add_pairs",
    )(ahead, back, parts, parts)


def end_pairs_kernel(a_ref, b_ref, part_ref, prefill_ref, decode_ref):
    half = prefill_ref.shape[0]
    total = a_ref[...].astype(jnp.float32) + b_ref[...].astype(jnp.float32)
    total += part_ref[0].astype(jnp.float32)
    prefill_ref[...] = total[:half]
    decode_ref[...] = total[half:]


def end_pairs(ahead, back, parts):
    _, rows, columns = parts.shape
    flat = pl.BlockSpec((rows, columns), lambda i: (0, 0))
    half = pl.BlockSpec((rows // 2, columns), lambda i: (0, 0))
    return pl.pallas_call(
        end_pairs_kernel,
        grid=(1,),
        in_specs=[flat, flat, pl.BlockSpec((1, rows, columns), lambda i: (0, 0, 0))],
        out_specs=[half, half],
        out_shape=[shaped((rows // 2, columns), jnp.float32)] * 2,
        compiler_params=VMEM,
        cost_estimate=cost(2 * rows * columns, 10 * rows * columns),
        name="end_pairs",
    )(ahead, back, parts)


def add_kernel(*refs):
    count = len(refs) // 3
    for arrived, part, out in zip(refs[:count], refs[count : 2 * count], refs[2 * count :]):
        out[...] = (arrived[...].astype(jnp.float32) + part[...].astype(jnp.float32)).astype(
            out.dtype
        )


def add_parts(arrived, parts):
    rows, columns = arrived[0].shape
    count = len(arrived)
    flat = pl.BlockSpec((rows, columns), lambda i: (0, 0))
    return pl.pallas_call(
        add_kernel,
        grid=(1,),
        in_specs=[flat] * (2 * count),
        out_specs=[flat] * count,
        out_shape=[shaped((rows, columns), jnp.bfloat16)] * count,
        compiler_params=VMEM,
        cost_estimate=cost(count * rows * columns, 6 * count * rows * columns),
        name="add_parts",
    )(*arrived, *parts)


def last_kernel(x_ref, *refs):
    terms, (mixed_ref, hidden_ref, square_ref) = (refs[:3], refs[3:6]), refs[6:]
    rows = refs[0].shape[0]
    sums = []
    for i in range(2):
        at = slice(i * rows, (i + 1) * rows)
        mixed = x_ref[at].astype(jnp.float32)
        for term in terms[i]:
            mixed += term[...].astype(jnp.float32)
        mixed_ref[at] = mixed
        hidden_ref[at] = mixed.astype(jnp.bfloat16)
        sums.append(jnp.sum(mixed * mixed, axis=1, keepdims=True))
    column = jnp.broadcast_to(jnp.concatenate(sums, axis=0), (2 * rows, 128))
    square_ref[...] = column.T[: square_ref.shape[0]]


def last_parts(x, prefill, decode):
    rows, columns = x.shape
    flat = pl.BlockSpec((rows, columns), lambda i: (0, 0))
    half = pl.BlockSpec((rows // 2, columns), lambda i: (0, 0))
    return pl.pallas_call(
        last_kernel,
        grid=(1,),
        in_specs=[flat] + [half] * 6,
        out_specs=[flat, flat, pl.BlockSpec((8, rows), lambda i: (0, 0))],
        out_shape=[
            shaped((rows, columns), jnp.float32),
            shaped((rows, columns), jnp.bfloat16),
            shaped((8, rows), jnp.float32),
        ],
        compiler_params=VMEM,
        cost_estimate=cost(4 * x.size, 12 * x.size),
        name="last_parts",
    )(x, *prefill, *decode)


def norm_kernel(width, mixed_ref, square_ref, gain_ref, out_ref):
    inv = lax.rsqrt(square_ref[...].T[:, :1] / width + EPS)
    out_ref[...] = (mixed_ref[...] * inv * gain_ref[...]).astype(jnp.bfloat16)


def norm_out(mixed, squares, gain, width):
    rows, columns = mixed.shape
    return pl.pallas_call(
        functools.partial(norm_kernel, width),
        grid=(1,),
        in_specs=[pl.BlockSpec(a.shape, lambda i: (0, 0)) for a in (mixed, squares, gain)],
        out_specs=pl.BlockSpec((rows, columns), lambda i: (0, 0)),
        out_shape=shaped((rows, columns), jnp.bfloat16),
        compiler_params=VMEM,
        cost_estimate=cost(3 * mixed.size, 6 * mixed.size),
        name="norm_out",
    )(mixed, squares, gain)


def query_kernel(count, first, last, width, blocks, *refs):
    gain_ref, w_ref, *refs = refs
    if not first:
        total_in, squares_in, *refs = refs
    if last:
        cos_ref, sin_ref, *refs = refs
        *pieces, q_ref, inv_ref, scaled, total, squares = refs
    else:
        *pieces, total, squares, scaled = refs
    each = len(pieces) // count
    step = pl.program_id(0)
    rows_each = pieces[0].shape[0]
    gain = gain_ref[...].astype(jnp.float32)

    @pl.when(step == 0)
    def _():
        total[...] = jnp.zeros_like(total) if first else total_in[...]
        squares[...] = jnp.zeros_like(squares) if first else squares_in[...]

    for k in range(count):

        @pl.when(step == k)
        def _(k=k):
            for i in range(each):
                rows = slice(i * rows_each, (i + 1) * rows_each)
                values = pieces[each * k + i][...].astype(jnp.float32)
                squares[rows] += jnp.sum(values * values, axis=1, keepdims=True)
                scaled[rows] = (values * gain).astype(jnp.bfloat16)

    total[...] += dot(scaled[...], w_ref[...])

    if last:

        @pl.when(step == count - 1)
        def _():
            inv = lax.rsqrt(squares[...] / width + EPS)
            inv_ref[...] = inv
            for head in range(q_ref.shape[1] // HEAD_SIZE):
                at = slice(head * HEAD_SIZE, (head + 1) * HEAD_SIZE)
                q_ref[:, at] = turned(total[:, at] * inv, cos_ref[...], sin_ref[...]).astype(
                    jnp.bfloat16
                )


def pick(places, k, blocks):
    block = blocks[places[0]]
    for i, place in enumerate(places[1:], 1):
        block = jnp.where(k == i, blocks[place], block)
    return block


def query_part(places, pieces, gain_row, weight, blocks, sums=None, angles=None, at=0):
    count = len(places)
    rows_each, depth = pieces[0].shape
    rows, width = len(pieces) // count * rows_each, weight.shape[1]
    first, last = sums is None, angles is not None
    whole = lambda shape, at=0: pl.BlockSpec(shape, lambda k, b: (at, 0))
    sum_shapes = [(rows, width), (rows, 1)]
    in_specs = [
        pl.BlockSpec((1, depth), lambda k, b: (0, pick(places, k, b))),
        pl.BlockSpec((depth, width), lambda k, b: (pick(places, k, b), 0)),
    ]
    operands = [gain_row, weight]
    if not first:
        in_specs += [whole(s, at) for s in sum_shapes]
        operands += sums
    scratch = [pltpu.VMEM((rows, depth), jnp.bfloat16)]
    if last:
        in_specs += [whole((rows, HEAD_SIZE))] * 2
        operands += angles
        scratch += [pltpu.VMEM(s, jnp.float32) for s in sum_shapes]
        out_shape = [shaped((rows, width), jnp.bfloat16), shaped((rows, 1), jnp.float32)]
    else:
        out_shape = [shaped(s, jnp.float32) for s in sum_shapes]
    return pl.pallas_call(
        functools.partial(query_kernel, count, first, last, weight.shape[0]),
        grid_spec=pltpu.PrefetchScalarGridSpec(
            num_scalar_prefetch=1,
            grid=(count,),
            in_specs=in_specs + [whole((rows_each, depth))] * len(pieces),
            out_specs=[whole(s) for s in sum_shapes],
            scratch_shapes=scratch,
        ),
        out_shape=out_shape,
        compiler_params=VMEM,
        cost_estimate=cost(2 * count * rows * depth * width, count * depth * width * 4),
        name="query_part",
    )(blocks, *operands, *pieces)


def new_pairs(pairs_ref, inv_ref, cos_ref, sin_ref):
    pairs = (pairs_ref[...] * inv_ref[...]).astype(jnp.bfloat16)
    keys = turned(pairs[:, :HEAD_SIZE].astype(jnp.float32), cos_ref[...], sin_ref[...])
    return keys.astype(jnp.bfloat16), pairs[:, HEAD_SIZE:]


def decode_kernel(
    q_ref, cache_ref, bias_ref, pairs_ref, inv_ref, cos_ref, sin_ref, out_ref, new_key, new_value
):
    @pl.when(pl.program_id(0) == 0)
    def _():
        keys, values = new_pairs(pairs_ref, inv_ref, cos_ref, sin_ref)
        new_key[...] = keys.astype(jnp.float32)
        new_value[...] = values.astype(jnp.float32)

    for head in range(q_ref.shape[1] // HEAD_SIZE):
        at = slice(head * HEAD_SIZE, (head + 1) * HEAD_SIZE)
        q = q_ref[:, at]
        score = dot_t(q, cache_ref[:, :HEAD_SIZE]) * FACTOR2 + bias_ref[...]
        own = jnp.sum(q.astype(jnp.float32) * new_key[...], axis=1, keepdims=True) * FACTOR2
        peak = jnp.maximum(jnp.max(score, axis=1, keepdims=True), own)
        grown, grown_own = jnp.exp2(score - peak), jnp.exp2(own - peak)
        scale = 1.0 / (jnp.sum(grown, axis=1, keepdims=True) + grown_own)
        context = dot(grown.astype(jnp.bfloat16), cache_ref[:, HEAD_SIZE:])
        out_ref[:, at] = ((context + grown_own * new_value[...]) * scale).astype(jnp.bfloat16)


def decode_context(q, cache, bias, pairs, inv, cosine, sine):
    rows, width = q.shape
    heads = min(4 * HEAD_SIZE, width)
    tokens = cache.shape[0]
    whole = lambda array: pl.BlockSpec(array.shape, lambda h: (0, 0))
    return pl.pallas_call(
        decode_kernel,
        grid=(width // heads,),
        in_specs=[pl.BlockSpec((rows, heads), lambda h: (0, h))]
        + [whole(a) for a in (cache, bias, pairs, inv, cosine, sine)],
        out_specs=pl.BlockSpec((rows, heads), lambda h: (0, h)),
        scratch_shapes=[
            pltpu.VMEM((rows, HEAD_SIZE), jnp.float32),
            pltpu.VMEM((rows, HEAD_SIZE), jnp.float32),
        ],
        out_shape=shaped((rows, width), jnp.bfloat16),
        compiler_params=VMEM,
        cost_estimate=cost(4 * rows * width * tokens, 8 * rows * width, 2 * width * tokens),
        name="decode_context",
    )(q, cache, bias, pairs, inv, cosine, sine)


def prefill_kernel(
    q_ref, prefix_ref, bias_ref, pairs_ref, inv_ref, cos_ref, sin_ref, out_ref, keys, values
):
    old = prefix_ref.shape[0]

    @pl.when(pl.program_id(0) == 0)
    def _():
        new_keys, new_values = new_pairs(pairs_ref, inv_ref, cos_ref, sin_ref)
        keys[:old] = prefix_ref[:, :HEAD_SIZE]
        keys[old:] = new_keys
        values[:old] = prefix_ref[:, HEAD_SIZE:]
        values[old:] = new_values

    for head in range(q_ref.shape[1] // HEAD_SIZE):
        at = slice(head * HEAD_SIZE, (head + 1) * HEAD_SIZE)
        score = dot_t(q_ref[:, at], keys[...]) * FACTOR2 + bias_ref[...]
        grown = jnp.exp2(score - jnp.max(score, axis=1, keepdims=True))
        scale = 1.0 / jnp.sum(grown, axis=1, keepdims=True)
        context = dot(grown.astype(jnp.bfloat16), values[...]) * scale
        out_ref[:, at] = context.astype(jnp.bfloat16)


def prefill_context(q, prefix, bias, pairs, inv, cosine, sine):
    rows, width = q.shape
    heads = min(4 * HEAD_SIZE, width)
    tokens = prefix.shape[0] + rows
    whole = lambda array: pl.BlockSpec(array.shape, lambda h: (0, 0))
    return pl.pallas_call(
        prefill_kernel,
        grid=(width // heads,),
        in_specs=[pl.BlockSpec((rows, heads), lambda h: (0, h))]
        + [whole(a) for a in (prefix, bias, pairs, inv, cosine, sine)],
        out_specs=pl.BlockSpec((rows, heads), lambda h: (0, h)),
        scratch_shapes=[
            pltpu.VMEM((tokens, HEAD_SIZE), jnp.bfloat16),
            pltpu.VMEM((tokens, HEAD_SIZE), jnp.bfloat16),
        ],
        out_shape=shaped((rows, width), jnp.bfloat16),
        compiler_params=VMEM,
        cost_estimate=cost(4 * rows * width * tokens, 8 * rows * width, 2 * width * tokens),
        name="prefill_context",
    )(q, prefix, bias, pairs, inv, cosine, sine)


def masks_kernel(
    page_size, request_ref, column_ref, owner_ref, page_ref, pos_ref, prefill_ref, decode_ref
):
    old = owner_ref.shape[1]
    rows = request_ref.shape[0]
    request = request_ref[...]
    prefill_ref[:, :old] = jnp.where(request == owner_ref[...], 0.0, NEGATIVE)
    row = lax.broadcasted_iota(jnp.int32, (rows, rows), 0)
    column = lax.broadcasted_iota(jnp.int32, (rows, rows), 1)
    allowed = (request == column_ref[...]) & (column <= row)
    prefill_ref[:, old:] = jnp.where(allowed, 0.0, NEGATIVE)

    token = lax.broadcasted_iota(jnp.int32, decode_ref.shape, 1)
    page, offset = token // page_size, token % page_size
    times = jnp.zeros(decode_ref.shape, jnp.float32)
    for j in range(page_ref.shape[1]):
        hit = (page == page_ref[:, j : j + 1]) & (offset + j * page_size < pos_ref[...])
        times += jnp.where(hit, 1.0, 0.0)
    decode_ref[...] = jnp.where(times > 0, jnp.log2(jnp.maximum(times, 1.0)), NEGATIVE)


def masks(request, owner, page_table, positions, tokens, page_size):
    rows, decode = request.shape[0], positions.shape[0]
    operands = (
        request[:, None], request[None, :], owner[None, :], page_table, positions[:, None]
    )
    outs = [(rows, owner.shape[0] + rows), (decode, tokens)]
    return pl.pallas_call(
        functools.partial(masks_kernel, page_size),
        grid=(1,),
        in_specs=[pl.BlockSpec(a.shape, lambda i: (0, 0)) for a in operands],
        out_specs=[pl.BlockSpec(a, lambda i: (0, 0)) for a in outs],
        out_shape=[shaped(a, jnp.float32) for a in outs],
        compiler_params=VMEM,
        cost_estimate=cost(20 * decode * tokens, 4 * decode * tokens),
        name="masks",
    )(*operands)


def output_kernel(count, jobs, blocks, *refs):
    contexts, weights, outs = refs[:count], refs[count : -len(jobs)], refs[-len(jobs) :]
    for (c, w), out in zip(jobs, outs):
        out[...] = dot(contexts[c][...], weights[w][...]).astype(jnp.bfloat16)


def output_part(contexts, weight, places, blocks, jobs=None, tiles=4):
    rows, depth = contexts[0].shape
    columns = weight.shape[1] // RING
    tile = columns // tiles
    count = len(contexts)
    jobs = jobs or [(c, w) for w in range(len(places)) for c in range(count)]
    return pl.pallas_call(
        functools.partial(output_kernel, count, tuple(jobs)),
        grid_spec=pltpu.PrefetchScalarGridSpec(
            num_scalar_prefetch=1,
            grid=(tiles,),
            in_specs=[pl.BlockSpec((rows, depth), lambda t, b: (0, 0))] * count
            + [pl.BlockSpec((depth, tile), lambda t, b, p=p: (0, b[p] * tiles + t)) for p in places],
            out_specs=[pl.BlockSpec((rows, tile), lambda t, b: (0, t))] * len(jobs),
        ),
        out_shape=[shaped((rows, columns), jnp.bfloat16)] * len(jobs),
        compiler_params=VMEM,
        cost_estimate=cost(
            2 * len(jobs) * rows * depth * columns, 2 * len(places) * depth * columns
        ),
        name="output_part",
    )(blocks, *contexts, *([weight] * len(places)))


def after(array, *others):
    return lax.optimization_barrier((array, *others))[0]


def hop(ahead, back):
    return lax.ppermute(ahead, "tensor", FORWARD), lax.ppermute(back, "tensor", BACKWARD)


def sum_squares(squares):
    def partner(other):
        return lax.ppermute(squares, "tensor", [(t, t ^ other) for t in range(RING)])

    squares = squares + partner(1)
    return squares + partner(2) + partner(4) + partner(6)


def body(
    inputs,
    entry_gain,
    exit_gain,
    query_weight,
    key_value_matrix,
    output_weight,
    page_pool,
    page_table,
    positions,
    request_lengths,
    prefix_pages,
    source_pages,
    target_pages,
):
    decode = page_table.shape[0]
    prefill = inputs.shape[0] - decode
    page_count, page_size, _ = page_pool.shape
    me = lax.axis_index("tensor")
    width = inputs.shape[1]
    per_device = query_weight.shape[1] // HEAD_SIZE
    group = me * per_device // (QUERY_HEADS // KEY_VALUE_HEADS)
    pair = 2 * HEAD_SIZE

    ring = lax.axis_size("tensor") == RING
    if ring:
        ahead, back = [inputs], [inputs]

        def gather_hop(*others):
            sent = ahead[-1], back[-1]
            if len(ahead) == FAR:
                sent = sent[0][:prefill], sent[1][prefill:]
            if others:
                sent = lax.optimization_barrier((*sent, *others))[:2]
            for pieces, arrived in zip((ahead, back), hop(*sent)):
                pieces.append(arrived)

        gather_hop()
        token = lax.ppermute(inputs[:16, :HEAD_SIZE], "replica", [(0, 1), (1, 0)])
        local = after(inputs, token)
        page_pool, positions, request_lengths, prefix_pages = lax.optimization_barrier(
            (page_pool, positions, request_lengths, prefix_pages, token)
        )[:4]

    own_pool = lax.dynamic_slice_in_dim(page_pool, group * pair, pair, 2)
    peer_pool = lax.ppermute(own_pool, "replica", [(0, 1), (1, 0)])
    prefix = prefix_pages[0]
    page_max = target_pages.shape[2]
    arrived = peer_pool[source_pages.reshape(-1)]
    usable = jnp.arange(page_max, dtype=jnp.int32)[None, :] < prefix[:, None]
    target = jnp.where(usable.reshape(-1), target_pages.reshape(-1), page_count)
    cache = own_pool.at[target].set(arrived, mode="drop").reshape(-1, pair)
    prefix_rows = arrived.reshape(-1, pair)
    slots = jnp.where(usable, jnp.arange(prefix.shape[0], dtype=jnp.int32)[:, None], -1)
    owner = jnp.repeat(slots.reshape(-1), page_size)

    request, span = span_layout(request_lengths[0], prefix, prefill, page_size)
    cosine, sine = tables(jnp.concatenate([span, positions]))
    angles = ((cosine[:prefill], sine[:prefill]), (cosine[prefill:], sine[prefill:]))
    bias = masks(request, owner, page_table, positions, cache.shape[0], page_size)
    gain_row = entry_gain[None, :]

    def attend_prefill(q, pairs, inv):
        return prefill_context(q, prefix_rows, bias[0], pairs, inv, *angles[0])

    def attend_decode(q, pairs, inv):
        return decode_context(q, cache, bias[1], pairs, inv, *angles[1])

    exit_row = lax.dynamic_slice_in_dim(exit_gain, me * width, width, 0)
    exit_row = exit_row.astype(jnp.float32)[None, :]

    if ring:
        place = jnp.where(me % 2 == 0, me // 2, RING - 1 - me // 2)
        places = (place + jnp.arange(RING, dtype=jnp.int32)) % RING
        blocks = jnp.where(places < RING // 2, 2 * places, 2 * (RING - places) - 1)
        parts, *moving = pairs_partial(local, gain_row, key_value_matrix, blocks)

        def query(places, sums=None, **more):
            pieces = [back[k] if k < FAR else ahead[RING - k] for k in places]
            return query_part(places, pieces, gain_row, query_weight, blocks, sums, **more)

        def query_end(pieces, which, sums):
            return query_part(
                (FAR,), pieces, gain_row, query_weight, blocks, sums, angles[which], which
            )

        def pairs_hop(moving, *others):
            return lax.optimization_barrier((*hop(*moving), *others))[:2]

        moving = add_pairs(*hop(*moving), parts, 3, 5)
        gather_hop(*moving)
        sums = query((0, 1, 7))
        moving = add_pairs(*pairs_hop(moving, sums[1]), parts, 2, 6)
        gather_hop(*moving)
        sums = query((2, 6), sums)
        moving = pairs_hop(moving, sums[1], cache, *bias, *angles[0], *angles[1])
        moving = add_pairs(*moving, parts, 1, 7)
        gather_hop(*moving)
        sums = query((3, 5), sums)
        pairs = end_pairs(*pairs_hop(moving, sums[1]), parts)

        q, inv = query_end([ahead[FAR]], 0, sums)
        prefilled = attend_prefill(q, pairs[0], inv)
        p4, p5 = output_part([prefilled], output_weight, (4, 5), blocks)
        p_ahead, p_back = hop(p4, p5)
        q, inv = query_end([back[FAR]], 1, sums)
        decoded = attend_decode(q, pairs[1], inv)
        d4, d3 = output_part(
            [lax.optimization_barrier((decoded, p_ahead, p_back))[0]], output_weight, (4, 3), blocks
        )
        d_ahead, d_back = hop(d3, d4)
        both = [prefilled, decoded]
        p3, d5 = output_part(both, output_weight, (3, 5), blocks, [(0, 0), (1, 1)])
        p6, d6, p2, d2 = output_part(both, output_weight, (6, 2), blocks)
        p_ahead, p_back = hop(*add_parts((p_ahead, p_back), (p3, p6)))
        d_ahead, d_back = hop(*add_parts((d_ahead, d_back), (d2, d5)))
        p7, d7, p1, d1 = output_part(both, output_weight, (7, 1), blocks)
        p_ahead, p_back = hop(*add_parts((p_ahead, p_back), (p2, p7)))
        d_ahead, d_back = hop(*add_parts((d_ahead, d_back), (d1, d6)))
        p0, d0 = output_part(both, output_weight, (0,), blocks)
        p_ahead = lax.ppermute(add_parts((p_ahead,), (p1,))[0], "tensor", FORWARD)
        d_back = lax.ppermute(add_parts((d_back,), (d7,))[0], "tensor", BACKWARD)
        mixed, hidden, squares = last_parts(inputs, (p_ahead, p_back, p0), (d_ahead, d_back, d0))
        return hidden, norm_out(mixed, sum_squares(squares), exit_row, exit_gain.shape[0])

    rows = lax.all_gather(inputs, "tensor", axis=1, tiled=True).astype(jnp.float32)
    inv = lax.rsqrt(jnp.mean(rows * rows, axis=1, keepdims=True) + EPS)
    scaled = (rows * inv * entry_gain.astype(jnp.float32)).astype(jnp.bfloat16)
    own = lax.dynamic_slice_in_dim(scaled, me * width, width, 1)
    pairs = lax.psum(dot(own, key_value_matrix), "tensor")
    pairs = lax.dynamic_slice_in_dim(pairs, group * pair, pair, 1)
    q = dot(scaled, query_weight).reshape(-1, per_device, HEAD_SIZE)
    swapped = jnp.roll(q, HEAD_SIZE // 2, 2)
    q = (q * cosine[:, None] + swapped * sine[:, None]).astype(jnp.bfloat16)
    q = q.reshape(-1, per_device * HEAD_SIZE)
    one = jnp.ones_like(inv)
    context = [
        attend_prefill(q[:prefill], pairs[:prefill], one[:prefill]),
        attend_decode(q[prefill:], pairs[prefill:], one[prefill:]),
    ]
    context = jnp.concatenate(context, axis=0)
    summed = lax.psum_scatter(
        dot(context, output_weight), "tensor", scatter_dimension=1, tiled=True
    )
    mixed = inputs.astype(jnp.float32) + summed
    squares = lax.psum(jnp.sum(mixed * mixed, axis=1), "tensor")[:, None]
    out = mixed * lax.rsqrt(squares / exit_gain.shape[0] + EPS) * exit_row
    return mixed.astype(jnp.bfloat16), out.astype(jnp.bfloat16)


def solution(mesh):
    rows = ("groups", "replica")
    return jax.shard_map(
        body,
        mesh=mesh,
        in_specs=(
            P(rows, "tensor"),
            P(),
            P(),
            P(None, "tensor"),
            P("tensor", None),
            P("tensor", None),
            P(rows, None, None),
            P(rows, None),
            P(rows),
            P(rows, None),
            P(rows, None),
            P(rows, None, None),
            P(rows, None, None),
        ),
        out_specs=(P(rows, "tensor"), P(rows, "tensor")),
        check_vma=False,
    )
```

```python
import functools
import math

import jax
import jax.numpy as jnp
import numpy as np
from jax import lax
from jax.experimental import pallas as pl
from jax.experimental.pallas import tpu as pltpu
from jax.sharding import PartitionSpec as P

QUERY_HEADS = 64
KEY_VALUE_HEADS = 8
HEAD_SIZE = 128
EPS = 1e-06
THETA = 1000000.0
NEGATIVE = -1e30
FACTOR2 = math.log2(math.e) / math.sqrt(HEAD_SIZE)

ORDER = (0, 2, 4, 6, 7, 5, 3, 1)
RING = len(ORDER)
FAR = RING // 2
FORWARD = [(ORDER[i], ORDER[(i + 1) % RING]) for i in range(RING)]
BACKWARD = [(b, a) for a, b in FORWARD]

VMEM = pltpu.CompilerParams(vmem_limit_bytes=48 * 1024 * 1024)


def dot(left, right):
    return jnp.dot(left, right, preferred_element_type=jnp.float32)


def dot_t(left, right):
    return lax.dot_general(
        left, right, (((1,), (1,)), ((), ())), preferred_element_type=jnp.float32
    )


def turned(values, cosine, sine):
    return values * cosine + pltpu.roll(values, HEAD_SIZE // 2, 1) * sine


def span_layout(lengths, prefix, prefill, page_size):
    request_end = jnp.cumsum(lengths)
    request_start = request_end - lengths
    token_index = jnp.arange(prefill, dtype=jnp.int32)
    request = jnp.sum((token_index[:, None] >= request_end[None, :]).astype(jnp.int32), axis=1)
    onehot = (request[:, None] == jnp.arange(lengths.shape[0], dtype=jnp.int32)[None, :]).astype(
        jnp.int32
    )
    token_start = jnp.sum(onehot * request_start[None, :], axis=1)
    token_prefix = jnp.sum(onehot * prefix[None, :], axis=1)
    return (request, token_prefix * page_size + token_index - token_start)


def tables(positions):
    half_dim = HEAD_SIZE // 2
    frequency = jnp.exp(
        jnp.arange(half_dim, dtype=jnp.float32) * (-2.0 * math.log(THETA) / HEAD_SIZE)
    )
    angles = positions.astype(jnp.float32)[:, None] * frequency[None, :]
    cosine, sine = jnp.cos(angles), jnp.sin(angles)
    return (
        jnp.concatenate([cosine, cosine], axis=1),
        jnp.concatenate([-sine, sine], axis=1),
    )


def cost(flops, moved, transcendentals=0):
    return pl.CostEstimate(flops=flops, bytes_accessed=moved, transcendentals=transcendentals)


def shaped(shape, dtype):
    return jax.ShapeDtypeStruct(shape, dtype)


def pairs_kernel(blocks, x_ref, gain_ref, w_ref, out_ref, forward_ref, backward_ref, scaled):
    k = pl.program_id(0)

    @pl.when(k == 0)
    def _():
        gain = gain_ref[...].astype(jnp.float32)
        scaled[...] = (x_ref[...].astype(jnp.float32) * gain).astype(jnp.bfloat16)

    result = dot(scaled[...], w_ref[...]).astype(jnp.bfloat16)
    out_ref[0] = result
    half = forward_ref.shape[0]

    @pl.when(k == FAR)
    def _():
        forward_ref[...] = result[:half]
        backward_ref[...] = result[half:]


def pairs_partial(x, gain_row, matrix, blocks):
    rows, width = x.shape
    columns = matrix.shape[1] // RING
    first = pl.BlockSpec((rows // 2, columns), lambda k, b: (0, 0))
    return pl.pallas_call(
        pairs_kernel,
        grid_spec=pltpu.PrefetchScalarGridSpec(
            num_scalar_prefetch=1,
            grid=(RING,),
            in_specs=[
                pl.BlockSpec((rows, width), lambda k, b: (0, 0)),
                pl.BlockSpec((1, width), lambda k, b: (0, b[0])),
                pl.BlockSpec((width, columns), lambda k, b: (0, b[k])),
            ],
            out_specs=[pl.BlockSpec((1, rows, columns), lambda k, b: (k, 0, 0)), first, first],
            scratch_shapes=[pltpu.VMEM((rows, width), jnp.bfloat16)],
        ),
        out_shape=[
            shaped((RING, rows, columns), jnp.bfloat16),
            shaped((rows // 2, columns), jnp.bfloat16),
            shaped((rows // 2, columns), jnp.bfloat16),
        ],
        compiler_params=VMEM,
        cost_estimate=cost(2 * x.size * matrix.shape[1], 2 * (x.size + 2 * matrix.size)),
        name="pairs_partial",
    )(blocks, x, gain_row, matrix)


def add_pairs_kernel(a_ref, b_ref, pa_ref, pb_ref, oa_ref, ob_ref):
    rows, half = oa_ref.shape[0], oa_ref.shape[0] // 2
    sides = ((a_ref, pa_ref, oa_ref, 0), (b_ref, pb_ref, ob_ref, half))
    for arrived, part, out, low in sides:
        if arrived.shape[0] == rows:
            total = arrived[...].astype(jnp.float32) + part[0].astype(jnp.float32)
            out[...] = total.astype(out.dtype)
        else:
            out[...] = part[0]
            at = slice(low, low + half)
            total = arrived[...].astype(jnp.float32) + part[0, at].astype(jnp.float32)
            out[at] = total.astype(out.dtype)


def add_pairs(ahead, back, parts, ka, kb):
    _, rows, columns = parts.shape
    whole = lambda array: pl.BlockSpec(array.shape, lambda i: (0, 0))
    flat = pl.BlockSpec((rows, columns), lambda i: (0, 0))
    return pl.pallas_call(
        add_pairs_kernel,
        grid=(1,),
        in_specs=[
            whole(ahead),
            whole(back),
            pl.BlockSpec((1, rows, columns), lambda i: (ka, 0, 0)),
            pl.BlockSpec((1, rows, columns), lambda i: (kb, 0, 0)),
        ],
        out_specs=[flat, flat],
        out_shape=[shaped((rows, columns), jnp.bfloat16)] * 2,
        compiler_params=VMEM,
        cost_estimate=cost(2 * rows * columns, 12 * rows * columns),
        name="add_pairs",
    )(ahead, back, parts, parts)


def end_pairs_kernel(a_ref, b_ref, part_ref, prefill_ref, decode_ref):
    half = prefill_ref.shape[0]
    total = a_ref[...].astype(jnp.float32) + b_ref[...].astype(jnp.float32)
    total += part_ref[0].astype(jnp.float32)
    prefill_ref[...] = total[:half]
    decode_ref[...] = total[half:]


def end_pairs(ahead, back, parts):
    _, rows, columns = parts.shape
    flat = pl.BlockSpec((rows, columns), lambda i: (0, 0))
    half = pl.BlockSpec((rows // 2, columns), lambda i: (0, 0))
    return pl.pallas_call(
        end_pairs_kernel,
        grid=(1,),
        in_specs=[flat, flat, pl.BlockSpec((1, rows, columns), lambda i: (0, 0, 0))],
        out_specs=[half, half],
        out_shape=[shaped((rows // 2, columns), jnp.float32)] * 2,
        compiler_params=VMEM,
        cost_estimate=cost(2 * rows * columns, 10 * rows * columns),
        name="end_pairs",
    )(ahead, back, parts)


def add_kernel(*refs):
    count = len(refs) // 3
    for arrived, part, out in zip(refs[:count], refs[count : 2 * count], refs[2 * count :]):
        out[...] = (arrived[...].astype(jnp.float32) + part[...].astype(jnp.float32)).astype(
            out.dtype
        )


def add_parts(arrived, parts):
    rows, columns = arrived[0].shape
    count = len(arrived)
    flat = pl.BlockSpec((rows, columns), lambda i: (0, 0))
    return pl.pallas_call(
        add_kernel,
        grid=(1,),
        in_specs=[flat] * (2 * count),
        out_specs=[flat] * count,
        out_shape=[shaped((rows, columns), jnp.bfloat16)] * count,
        compiler_params=VMEM,
        cost_estimate=cost(count * rows * columns, 6 * count * rows * columns),
        name="add_parts",
    )(*arrived, *parts)


def last_kernel(x_ref, *refs):
    terms, (mixed_ref, hidden_ref, square_ref) = (refs[:3], refs[3:6]), refs[6:]
    rows = refs[0].shape[0]
    sums = []
    for i in range(2):
        at = slice(i * rows, (i + 1) * rows)
        mixed = x_ref[at].astype(jnp.float32)
        for term in terms[i]:
            mixed += term[...].astype(jnp.float32)
        mixed_ref[at] = mixed
        hidden_ref[at] = mixed.astype(jnp.bfloat16)
        sums.append(jnp.sum(mixed * mixed, axis=1, keepdims=True))
    column = jnp.broadcast_to(jnp.concatenate(sums, axis=0), (2 * rows, 128))
    square_ref[...] = column.T[: square_ref.shape[0]]


def last_parts(x, prefill, decode):
    rows, columns = x.shape
    flat = pl.BlockSpec((rows, columns), lambda i: (0, 0))
    half = pl.BlockSpec((rows // 2, columns), lambda i: (0, 0))
    return pl.pallas_call(
        last_kernel,
        grid=(1,),
        in_specs=[flat] + [half] * 6,
        out_specs=[flat, flat, pl.BlockSpec((8, rows), lambda i: (0, 0))],
        out_shape=[
            shaped((rows, columns), jnp.float32),
            shaped((rows, columns), jnp.bfloat16),
            shaped((8, rows), jnp.float32),
        ],
        compiler_params=VMEM,
        cost_estimate=cost(4 * x.size, 12 * x.size),
        name="last_parts",
    )(x, *prefill, *decode)


def norm_kernel(width, mixed_ref, square_ref, gain_ref, out_ref):
    inv = lax.rsqrt(square_ref[...].T[:, :1] / width + EPS)
    out_ref[...] = (mixed_ref[...] * inv * gain_ref[...]).astype(jnp.bfloat16)


def norm_out(mixed, squares, gain, width):
    rows, columns = mixed.shape
    block = pl.BlockSpec((128, columns), lambda i: (i, 0))
    return pl.pallas_call(
        functools.partial(norm_kernel, width),
        grid=(rows // 128,),
        in_specs=[
            block,
            pl.BlockSpec((8, 128), lambda i: (0, i)),
            pl.BlockSpec((1, columns), lambda i: (0, 0)),
        ],
        out_specs=block,
        out_shape=shaped((rows, columns), jnp.bfloat16),
        compiler_params=VMEM,
        cost_estimate=cost(3 * mixed.size, 6 * mixed.size),
        name="norm_out",
    )(mixed, squares, gain)


def query_kernel(count, first, last, width, blocks, *refs):
    gain_ref, w_ref, *refs = refs
    if not first:
        total_in, squares_in, *refs = refs
    if last:
        cos_ref, sin_ref, *refs = refs
        *pieces, q_ref, inv_ref, scaled, total, squares = refs
    else:
        *pieces, total, squares, scaled = refs
    each = len(pieces) // count
    step = pl.program_id(0)
    rows_each = pieces[0].shape[0]
    gain = gain_ref[...].astype(jnp.float32)

    @pl.when(step == 0)
    def _():
        total[...] = jnp.zeros_like(total) if first else total_in[...]
        squares[...] = jnp.zeros_like(squares) if first else squares_in[...]

    for k in range(count):

        @pl.when(step == k)
        def _(k=k):
            for i in range(each):
                rows = slice(i * rows_each, (i + 1) * rows_each)
                values = pieces[each * k + i][...].astype(jnp.float32)
                squares[rows] += jnp.sum(values * values, axis=1, keepdims=True)
                scaled[rows] = (values * gain).astype(jnp.bfloat16)

    total[...] += dot(scaled[...], w_ref[...])

    if last:

        @pl.when(step == count - 1)
        def _():
            inv = lax.rsqrt(squares[...] / width + EPS)
            inv_ref[...] = inv
            for head in range(q_ref.shape[1] // HEAD_SIZE):
                at = slice(head * HEAD_SIZE, (head + 1) * HEAD_SIZE)
                q_ref[:, at] = turned(total[:, at] * inv, cos_ref[...], sin_ref[...]).astype(
                    jnp.bfloat16
                )


def pick(places, k, blocks):
    block = blocks[places[0]]
    for i, place in enumerate(places[1:], 1):
        block = jnp.where(k == i, blocks[place], block)
    return block


def query_part(places, pieces, gain_row, weight, blocks, sums=None, angles=None, at=0):
    count = len(places)
    rows_each, depth = pieces[0].shape
    rows, width = len(pieces) // count * rows_each, weight.shape[1]
    first, last = sums is None, angles is not None
    whole = lambda shape, at=0: pl.BlockSpec(shape, lambda k, b: (at, 0))
    sum_shapes = [(rows, width), (rows, 1)]
    in_specs = [
        pl.BlockSpec((1, depth), lambda k, b: (0, pick(places, k, b))),
        pl.BlockSpec((depth, width), lambda k, b: (pick(places, k, b), 0)),
    ]
    operands = [gain_row, weight]
    if not first:
        in_specs += [whole(s, at) for s in sum_shapes]
        operands += sums
    scratch = [pltpu.VMEM((rows, depth), jnp.bfloat16)]
    if last:
        in_specs += [whole((rows, HEAD_SIZE))] * 2
        operands += angles
        scratch += [pltpu.VMEM(s, jnp.float32) for s in sum_shapes]
        out_shape = [shaped((rows, width), jnp.bfloat16), shaped((rows, 1), jnp.float32)]
    else:
        out_shape = [shaped(s, jnp.float32) for s in sum_shapes]
    return pl.pallas_call(
        functools.partial(query_kernel, count, first, last, weight.shape[0]),
        grid_spec=pltpu.PrefetchScalarGridSpec(
            num_scalar_prefetch=1,
            grid=(count,),
            in_specs=in_specs + [whole((rows_each, depth))] * len(pieces),
            out_specs=[whole(s) for s in sum_shapes],
            scratch_shapes=scratch,
        ),
        out_shape=out_shape,
        compiler_params=VMEM,
        cost_estimate=cost(2 * count * rows * depth * width, count * depth * width * 4),
        name="query_part",
    )(blocks, *operands, *pieces)


def new_pairs(pairs_ref, inv_ref, cos_ref, sin_ref):
    pairs = (pairs_ref[...] * inv_ref[...]).astype(jnp.bfloat16)
    keys = turned(pairs[:, :HEAD_SIZE].astype(jnp.float32), cos_ref[...], sin_ref[...])
    return keys.astype(jnp.bfloat16), pairs[:, HEAD_SIZE:]


def weight_copies(places, blocks, weight, held, sems):
    columns = held.shape[2]
    return [
        pltpu.make_async_copy(
            weight.at[:, pl.ds(pl.multiple_of(blocks[place] * columns, columns), columns)],
            held.at[i],
            sems.at[i],
        )
        for i, place in enumerate(places)
    ]


def head_columns(ref):
    return [slice(low, low + HEAD_SIZE) for low in range(0, ref.shape[1], HEAD_SIZE)]


def decode_heads(refs, out_ref):
    q_ref, cache_ref, bias_ref, *rest = refs
    keys, values = new_pairs(*rest)
    keys, values = keys.astype(jnp.float32), values.astype(jnp.float32)
    for at in head_columns(out_ref):
        q = q_ref[:, at]
        score = dot_t(q, cache_ref[:, :HEAD_SIZE]) * FACTOR2 + bias_ref[...]
        own = jnp.sum(q.astype(jnp.float32) * keys, axis=1, keepdims=True) * FACTOR2
        peak = jnp.maximum(jnp.max(score, axis=1, keepdims=True), own)
        grown, grown_own = jnp.exp2(score - peak), jnp.exp2(own - peak)
        scale = 1.0 / (jnp.sum(grown, axis=1, keepdims=True) + grown_own)
        context = dot(grown.astype(jnp.bfloat16), cache_ref[:, HEAD_SIZE:])
        out_ref[:, at] = ((context + grown_own * values) * scale).astype(jnp.bfloat16)


def prefill_heads(refs, out_ref):
    q_ref, prefix_ref, bias_ref, *rest = refs
    new_keys, new_values = new_pairs(*rest)
    keys = jnp.concatenate([prefix_ref[:, :HEAD_SIZE], new_keys], axis=0)
    values = jnp.concatenate([prefix_ref[:, HEAD_SIZE:], new_values], axis=0)
    for at in head_columns(out_ref):
        score = dot_t(q_ref[:, at], keys) * FACTOR2 + bias_ref[...]
        grown = jnp.exp2(score - jnp.max(score, axis=1, keepdims=True))
        scale = 1.0 / jnp.sum(grown, axis=1, keepdims=True)
        context = dot(grown.astype(jnp.bfloat16), values) * scale
        out_ref[:, at] = context.astype(jnp.bfloat16)


def context_kernel(heads, places, blocks, *refs):
    if not places:
        heads(refs[:-1], refs[-1])
        return
    *refs, weight, out_ref, first, second, held, sems = refs
    copies = weight_copies(places, blocks, weight, held, sems)
    for copy in copies:
        copy.start()
    heads(refs, out_ref)
    tile = first.shape[1] // 4
    for i, (copy, product) in enumerate(zip(copies, (first, second))):
        copy.wait()
        for low in range(0, product.shape[1], tile):
            at = slice(low, low + tile)
            product[:, at] = dot(out_ref[...], held[i, :, at]).astype(jnp.bfloat16)


def contexts(heads, q, pages, bias, pairs, inv, angles, blocks, weight=None, places=()):
    rows, width = q.shape
    operands = [q, pages, bias, pairs, inv, *angles]
    in_specs = [pl.BlockSpec(a.shape, lambda i, b: (0, 0)) for a in operands]
    out_shape = [shaped((rows, width), jnp.bfloat16)]
    scratch = []
    if places:
        operands.append(weight)
        in_specs.append(pl.BlockSpec(memory_space=pl.ANY))
        columns = weight.shape[1] // RING
        out_shape += [shaped((rows, columns), jnp.bfloat16)] * 2
        scratch = [
            pltpu.VMEM((2, width, columns), jnp.bfloat16),
            pltpu.SemaphoreType.DMA((2,)),
        ]
    return pl.pallas_call(
        functools.partial(context_kernel, heads, places),
        grid_spec=pltpu.PrefetchScalarGridSpec(
            num_scalar_prefetch=1,
            grid=(1,),
            in_specs=in_specs,
            out_specs=[pl.BlockSpec(a.shape, lambda i, b: (0, 0)) for a in out_shape],
            scratch_shapes=scratch,
        ),
        out_shape=out_shape,
        compiler_params=VMEM,
        cost_estimate=cost(8 * rows * width * bias.shape[1], 16 * rows * width),
        name="contexts",
    )(blocks, *operands)


def masks_kernel(
    page_size, request_ref, column_ref, owner_ref, page_ref, pos_ref, prefill_ref, decode_ref
):
    old = owner_ref.shape[1]
    rows = request_ref.shape[0]
    request = request_ref[...]
    prefill_ref[:, :old] = jnp.where(request == owner_ref[...], 0.0, NEGATIVE)
    row = lax.broadcasted_iota(jnp.int32, (rows, rows), 0)
    column = lax.broadcasted_iota(jnp.int32, (rows, rows), 1)
    allowed = (request == column_ref[...]) & (column <= row)
    prefill_ref[:, old:] = jnp.where(allowed, 0.0, NEGATIVE)

    token = lax.broadcasted_iota(jnp.int32, decode_ref.shape, 1)
    page, offset = token // page_size, token % page_size
    times = jnp.zeros(decode_ref.shape, jnp.float32)
    for j in range(page_ref.shape[1]):
        hit = (page == page_ref[:, j : j + 1]) & (offset + j * page_size < pos_ref[...])
        times += jnp.where(hit, 1.0, 0.0)
    decode_ref[...] = jnp.where(times > 0, jnp.log2(jnp.maximum(times, 1.0)), NEGATIVE)


def masks(request, owner, page_table, positions, tokens, page_size):
    rows, decode = request.shape[0], positions.shape[0]
    operands = (
        request[:, None], request[None, :], owner[None, :], page_table, positions[:, None]
    )
    outs = [(rows, owner.shape[0] + rows), (decode, tokens)]
    return pl.pallas_call(
        functools.partial(masks_kernel, page_size),
        grid=(1,),
        in_specs=[pl.BlockSpec(a.shape, lambda i: (0, 0)) for a in operands],
        out_specs=[pl.BlockSpec(a, lambda i: (0, 0)) for a in outs],
        out_shape=[shaped(a, jnp.float32) for a in outs],
        compiler_params=VMEM,
        cost_estimate=cost(20 * decode * tokens, 4 * decode * tokens),
        name="masks",
    )(*operands)


def output_kernel(count, jobs, blocks, *refs):
    contexts, weights, outs = refs[:count], refs[count : -len(jobs)], refs[-len(jobs) :]
    for (c, w), out in zip(jobs, outs):
        out[...] = dot(contexts[c][...], weights[w][...]).astype(jnp.bfloat16)


def output_part(contexts, weight, places, blocks, jobs=None, tiles=4):
    rows, depth = contexts[0].shape
    columns = weight.shape[1] // RING
    tile = columns // tiles
    count = len(contexts)
    jobs = jobs or [(c, w) for w in range(len(places)) for c in range(count)]
    return pl.pallas_call(
        functools.partial(output_kernel, count, tuple(jobs)),
        grid_spec=pltpu.PrefetchScalarGridSpec(
            num_scalar_prefetch=1,
            grid=(tiles,),
            in_specs=[pl.BlockSpec((rows, depth), lambda t, b: (0, 0))] * count
            + [pl.BlockSpec((depth, tile), lambda t, b, p=p: (0, b[p] * tiles + t)) for p in places],
            out_specs=[pl.BlockSpec((rows, tile), lambda t, b: (0, t))] * len(jobs),
        ),
        out_shape=[shaped((rows, columns), jnp.bfloat16)] * len(jobs),
        compiler_params=VMEM,
        cost_estimate=cost(
            2 * len(jobs) * rows * depth * columns, 2 * len(places) * depth * columns
        ),
        name="output_part",
    )(blocks, *contexts, *([weight] * len(places)))


def after(array, *others):
    return lax.optimization_barrier((array, *others))[0]


def hop(ahead, back):
    return lax.ppermute(ahead, "tensor", FORWARD), lax.ppermute(back, "tensor", BACKWARD)


def sum_squares(squares):
    def partner(other):
        return lax.ppermute(squares, "tensor", [(t, t ^ other) for t in range(RING)])

    squares = squares + partner(1)
    return squares + partner(2) + partner(4) + partner(6)


def body(
    inputs,
    entry_gain,
    exit_gain,
    query_weight,
    key_value_matrix,
    output_weight,
    page_pool,
    page_table,
    positions,
    request_lengths,
    prefix_pages,
    source_pages,
    target_pages,
):
    decode = page_table.shape[0]
    prefill = inputs.shape[0] - decode
    page_count, page_size, _ = page_pool.shape
    me = lax.axis_index("tensor")
    width = inputs.shape[1]
    per_device = query_weight.shape[1] // HEAD_SIZE
    group = me * per_device // (QUERY_HEADS // KEY_VALUE_HEADS)
    pair = 2 * HEAD_SIZE

    ring = lax.axis_size("tensor") == RING
    if ring:
        ahead, back = [inputs], [inputs]

        def gather_hop(*others):
            sent = ahead[-1], back[-1]
            if len(ahead) == FAR:
                sent = sent[0][:prefill], sent[1][prefill:]
            if others:
                sent = lax.optimization_barrier((*sent, *others))[:2]
            for pieces, arrived in zip((ahead, back), hop(*sent)):
                pieces.append(arrived)

        gather_hop()
        token = lax.ppermute(inputs[:16, :HEAD_SIZE], "replica", [(0, 1), (1, 0)])
        local = after(inputs, token)
        page_pool, positions, request_lengths, prefix_pages = lax.optimization_barrier(
            (page_pool, positions, request_lengths, prefix_pages, token)
        )[:4]

    own_pool = lax.dynamic_slice_in_dim(page_pool, group * pair, pair, 2)
    peer_pool = lax.ppermute(own_pool, "replica", [(0, 1), (1, 0)])
    prefix = prefix_pages[0]
    page_max = target_pages.shape[2]
    arrived = peer_pool[source_pages.reshape(-1)]
    usable = jnp.arange(page_max, dtype=jnp.int32)[None, :] < prefix[:, None]
    target = jnp.where(usable.reshape(-1), target_pages.reshape(-1), page_count)
    cache = own_pool.at[target].set(arrived, mode="drop").reshape(-1, pair)
    prefix_rows = arrived.reshape(-1, pair)
    slots = jnp.where(usable, jnp.arange(prefix.shape[0], dtype=jnp.int32)[:, None], -1)
    owner = jnp.repeat(slots.reshape(-1), page_size)

    request, span = span_layout(request_lengths[0], prefix, prefill, page_size)
    cosine, sine = tables(jnp.concatenate([span, positions]))
    angles = ((cosine[:prefill], sine[:prefill]), (cosine[prefill:], sine[prefill:]))
    bias = masks(request, owner, page_table, positions, cache.shape[0], page_size)
    gain_row = entry_gain[None, :]

    def attend(which, q, pairs, inv, blocks, *product):
        heads, pages = ((prefill_heads, prefix_rows), (decode_heads, cache))[which]
        return contexts(heads, q, pages, bias[which], pairs, inv, angles[which], blocks, *product)

    exit_row = lax.dynamic_slice_in_dim(exit_gain, me * width, width, 0)
    exit_row = exit_row.astype(jnp.float32)[None, :]

    if ring:
        place = jnp.where(me % 2 == 0, me // 2, RING - 1 - me // 2)
        places = (place + jnp.arange(RING, dtype=jnp.int32)) % RING
        blocks = jnp.where(places < RING // 2, 2 * places, 2 * (RING - places) - 1)
        parts, *moving = pairs_partial(local, gain_row, key_value_matrix, blocks)

        def query(places, sums=None, **more):
            pieces = [back[k] if k < FAR else ahead[RING - k] for k in places]
            return query_part(places, pieces, gain_row, query_weight, blocks, sums, **more)

        def query_end(pieces, which, sums):
            return query_part(
                (FAR,), pieces, gain_row, query_weight, blocks, sums, angles[which], which
            )

        def settled(arrived, *others):
            return lax.optimization_barrier((*arrived, *others))[:2]

        arrived = hop(*moving)
        gather_hop()
        moving = add_pairs(*settled(arrived, ahead[1], back[1]), parts, 3, 5)
        sums = query((0, 1, 7))
        arrived = hop(*moving)
        gather_hop(*moving, sums[1])
        sums = query((2, 6), sums)
        moving = add_pairs(
            *settled(arrived, sums[1], cache, *bias, *angles[0], *angles[1]), parts, 2, 6
        )
        arrived = hop(*moving)
        gather_hop(*moving)
        moving = add_pairs(*settled(arrived, ahead[3], back[3]), parts, 1, 7)
        sums = query((3, 5), sums)
        pairs = end_pairs(*settled(hop(*moving), sums[1]), parts)

        q, inv = query_end([ahead[FAR]], 0, sums)
        prefilled, p4, p5 = attend(0, q, pairs[0], inv, blocks, output_weight, (4, 5))
        p_ahead, p_back = hop(p4, p5)
        q, inv = query_end([back[FAR]], 1, sums)
        q = after(q, p4)
        decoded, d4, d3 = attend(1, q, pairs[1], inv, blocks, output_weight, (4, 3))
        decoded, p_ahead, p_back = lax.optimization_barrier((decoded, p_ahead, p_back))
        d_ahead, d_back = hop(d3, d4)
        both = [prefilled, decoded]
        p3, d5 = output_part(both, output_weight, (3, 5), blocks, [(0, 0), (1, 1)])
        p6, d6, p2, d2 = output_part(both, output_weight, (6, 2), blocks)
        p_ahead, p_back = hop(*add_parts((p_ahead, p_back), (p3, p6)))
        d_ahead, d_back = hop(*add_parts((d_ahead, d_back), (d2, d5)))
        p7, d7, p1, d1 = output_part(both, output_weight, (7, 1), blocks)
        p_ahead, p_back = hop(*add_parts((p_ahead, p_back), (p2, p7)))
        d_ahead, d_back = hop(*add_parts((d_ahead, d_back), (d1, d6)))
        p0, d0 = output_part(both, output_weight, (0,), blocks)
        p_ahead = lax.ppermute(add_parts((p_ahead,), (p1,))[0], "tensor", FORWARD)
        d_back = lax.ppermute(add_parts((d_back,), (d7,))[0], "tensor", BACKWARD)
        mixed, hidden, squares = last_parts(inputs, (p_ahead, p_back, p0), (d_ahead, d_back, d0))
        return hidden, norm_out(mixed, sum_squares(squares), exit_row, exit_gain.shape[0])

    rows = lax.all_gather(inputs, "tensor", axis=1, tiled=True).astype(jnp.float32)
    inv = lax.rsqrt(jnp.mean(rows * rows, axis=1, keepdims=True) + EPS)
    scaled = (rows * inv * entry_gain.astype(jnp.float32)).astype(jnp.bfloat16)
    own = lax.dynamic_slice_in_dim(scaled, me * width, width, 1)
    pairs = lax.psum(dot(own, key_value_matrix), "tensor")
    pairs = lax.dynamic_slice_in_dim(pairs, group * pair, pair, 1)
    q = dot(scaled, query_weight).reshape(-1, per_device, HEAD_SIZE)
    swapped = jnp.roll(q, HEAD_SIZE // 2, 2)
    q = (q * cosine[:, None] + swapped * sine[:, None]).astype(jnp.bfloat16)
    q = q.reshape(-1, per_device * HEAD_SIZE)
    one = jnp.ones_like(inv)
    none = jnp.zeros((1,), jnp.int32)
    context = [
        attend(0, q[:prefill], pairs[:prefill], one[:prefill], none)[0],
        attend(1, q[prefill:], pairs[prefill:], one[prefill:], none)[0],
    ]
    context = jnp.concatenate(context, axis=0)
    summed = lax.psum_scatter(
        dot(context, output_weight), "tensor", scatter_dimension=1, tiled=True
    )
    mixed = inputs.astype(jnp.float32) + summed
    squares = lax.psum(jnp.sum(mixed * mixed, axis=1), "tensor")[:, None]
    out = mixed * lax.rsqrt(squares / exit_gain.shape[0] + EPS) * exit_row
    return mixed.astype(jnp.bfloat16), out.astype(jnp.bfloat16)


def solution(mesh):
    rows = ("groups", "replica")
    return jax.shard_map(
        body,
        mesh=mesh,
        in_specs=(
            P(rows, "tensor"),
            P(),
            P(),
            P(None, "tensor"),
            P("tensor", None),
            P("tensor", None),
            P(rows, None, None),
            P(rows, None),
            P(rows),
            P(rows, None),
            P(rows, None),
            P(rows, None, None),
            P(rows, None, None),
        ),
        out_specs=(P(rows, "tensor"), P(rows, "tensor")),
        check_vma=False,
    )
```

```python
import functools
import math

import jax
import jax.numpy as jnp
import numpy as np
from jax import lax
from jax.experimental import pallas as pl
from jax.experimental.pallas import tpu as pltpu
from jax.sharding import PartitionSpec as P

QUERY_HEADS = 64
KEY_VALUE_HEADS = 8
HEAD_SIZE = 128
EPS = 1e-06
THETA = 1000000.0
NEGATIVE = -1e30
FACTOR2 = math.log2(math.e) / math.sqrt(HEAD_SIZE)

ORDER = (0, 2, 4, 6, 7, 5, 3, 1)
RING = len(ORDER)
FAR = RING // 2
FORWARD = [(ORDER[i], ORDER[(i + 1) % RING]) for i in range(RING)]
BACKWARD = [(b, a) for a, b in FORWARD]

VMEM = pltpu.CompilerParams(vmem_limit_bytes=48 * 1024 * 1024)


def dot(left, right):
    return jnp.dot(left, right, preferred_element_type=jnp.float32)


def dot_t(left, right):
    return lax.dot_general(
        left, right, (((1,), (1,)), ((), ())), preferred_element_type=jnp.float32
    )


def turned(values, cosine, sine):
    return values * cosine + pltpu.roll(values, HEAD_SIZE // 2, 1) * sine


def span_layout(lengths, prefix, prefill, page_size):
    request_end = jnp.cumsum(lengths)
    request_start = request_end - lengths
    token_index = jnp.arange(prefill, dtype=jnp.int32)
    request = jnp.sum((token_index[:, None] >= request_end[None, :]).astype(jnp.int32), axis=1)
    onehot = (request[:, None] == jnp.arange(lengths.shape[0], dtype=jnp.int32)[None, :]).astype(
        jnp.int32
    )
    token_start = jnp.sum(onehot * request_start[None, :], axis=1)
    token_prefix = jnp.sum(onehot * prefix[None, :], axis=1)
    return (request, token_prefix * page_size + token_index - token_start)


def tables(positions):
    half_dim = HEAD_SIZE // 2
    frequency = jnp.exp(
        jnp.arange(half_dim, dtype=jnp.float32) * (-2.0 * math.log(THETA) / HEAD_SIZE)
    )
    angles = positions.astype(jnp.float32)[:, None] * frequency[None, :]
    cosine, sine = jnp.cos(angles), jnp.sin(angles)
    return (
        jnp.concatenate([cosine, cosine], axis=1),
        jnp.concatenate([-sine, sine], axis=1),
    )


def cost(flops, moved, transcendentals=0):
    return pl.CostEstimate(flops=flops, bytes_accessed=moved, transcendentals=transcendentals)


def shaped(shape, dtype):
    return jax.ShapeDtypeStruct(shape, dtype)


def pairs_kernel(blocks, x_ref, gain_ref, w_ref, out_ref, forward_ref, backward_ref, scaled):
    k = pl.program_id(0)

    @pl.when(k == 0)
    def _():
        gain = gain_ref[...].astype(jnp.float32)
        scaled[...] = (x_ref[...].astype(jnp.float32) * gain).astype(jnp.bfloat16)

    result = dot(scaled[...], w_ref[...]).astype(jnp.bfloat16)
    out_ref[0] = result
    half = forward_ref.shape[0]

    @pl.when(k == FAR)
    def _():
        forward_ref[...] = result[:half]
        backward_ref[...] = result[half:]


def pairs_partial(x, gain_row, matrix, blocks):
    rows, width = x.shape
    columns = matrix.shape[1] // RING
    first = pl.BlockSpec((rows // 2, columns), lambda k, b: (0, 0))
    return pl.pallas_call(
        pairs_kernel,
        grid_spec=pltpu.PrefetchScalarGridSpec(
            num_scalar_prefetch=1,
            grid=(RING,),
            in_specs=[
                pl.BlockSpec((rows, width), lambda k, b: (0, 0)),
                pl.BlockSpec((1, width), lambda k, b: (0, b[0])),
                pl.BlockSpec((width, columns), lambda k, b: (0, b[k])),
            ],
            out_specs=[pl.BlockSpec((1, rows, columns), lambda k, b: (k, 0, 0)), first, first],
            scratch_shapes=[pltpu.VMEM((rows, width), jnp.bfloat16)],
        ),
        out_shape=[
            shaped((RING, rows, columns), jnp.bfloat16),
            shaped((rows // 2, columns), jnp.bfloat16),
            shaped((rows // 2, columns), jnp.bfloat16),
        ],
        compiler_params=VMEM,
        cost_estimate=cost(2 * x.size * matrix.shape[1], 2 * (x.size + 2 * matrix.size)),
        name="pairs_partial",
    )(blocks, x, gain_row, matrix)


def add_pairs_kernel(a_ref, b_ref, pa_ref, pb_ref, oa_ref, ob_ref):
    rows, half = oa_ref.shape[0], oa_ref.shape[0] // 2
    sides = ((a_ref, pa_ref, oa_ref, 0), (b_ref, pb_ref, ob_ref, half))
    for arrived, part, out, low in sides:
        if arrived.shape[0] == rows:
            total = arrived[...].astype(jnp.float32) + part[0].astype(jnp.float32)
            out[...] = total.astype(out.dtype)
        else:
            out[...] = part[0]
            at = slice(low, low + half)
            total = arrived[...].astype(jnp.float32) + part[0, at].astype(jnp.float32)
            out[at] = total.astype(out.dtype)


def add_pairs(ahead, back, parts, ka, kb):
    _, rows, columns = parts.shape
    whole = lambda array: pl.BlockSpec(array.shape, lambda i: (0, 0))
    flat = pl.BlockSpec((rows, columns), lambda i: (0, 0))
    return pl.pallas_call(
        add_pairs_kernel,
        grid=(1,),
        in_specs=[
            whole(ahead),
            whole(back),
            pl.BlockSpec((1, rows, columns), lambda i: (ka, 0, 0)),
            pl.BlockSpec((1, rows, columns), lambda i: (kb, 0, 0)),
        ],
        out_specs=[flat, flat],
        out_shape=[shaped((rows, columns), jnp.bfloat16)] * 2,
        compiler_params=VMEM,
        cost_estimate=cost(2 * rows * columns, 12 * rows * columns),
        name="add_pairs",
    )(ahead, back, parts, parts)


def end_pairs_kernel(a_ref, b_ref, part_ref, prefill_ref, decode_ref):
    half = prefill_ref.shape[0]
    total = a_ref[...].astype(jnp.float32) + b_ref[...].astype(jnp.float32)
    total += part_ref[0].astype(jnp.float32)
    prefill_ref[...] = total[:half]
    decode_ref[...] = total[half:]


def end_pairs(ahead, back, parts):
    _, rows, columns = parts.shape
    flat = pl.BlockSpec((rows, columns), lambda i: (0, 0))
    half = pl.BlockSpec((rows // 2, columns), lambda i: (0, 0))
    return pl.pallas_call(
        end_pairs_kernel,
        grid=(1,),
        in_specs=[flat, flat, pl.BlockSpec((1, rows, columns), lambda i: (0, 0, 0))],
        out_specs=[half, half],
        out_shape=[shaped((rows // 2, columns), jnp.float32)] * 2,
        compiler_params=VMEM,
        cost_estimate=cost(2 * rows * columns, 10 * rows * columns),
        name="end_pairs",
    )(ahead, back, parts)


def add_kernel(*refs):
    count = len(refs) // 3
    for arrived, part, out in zip(refs[:count], refs[count : 2 * count], refs[2 * count :]):
        out[...] = (arrived[...].astype(jnp.float32) + part[...].astype(jnp.float32)).astype(
            out.dtype
        )


def add_parts(arrived, parts):
    rows, columns = arrived[0].shape
    count = len(arrived)
    flat = pl.BlockSpec((rows, columns), lambda i: (0, 0))
    return pl.pallas_call(
        add_kernel,
        grid=(1,),
        in_specs=[flat] * (2 * count),
        out_specs=[flat] * count,
        out_shape=[shaped((rows, columns), jnp.bfloat16)] * count,
        compiler_params=VMEM,
        cost_estimate=cost(count * rows * columns, 6 * count * rows * columns),
        name="add_parts",
    )(*arrived, *parts)


def last_kernel(x_ref, *refs):
    terms, (mixed_ref, hidden_ref, square_ref) = (refs[:3], refs[3:6]), refs[6:]
    rows = refs[0].shape[0]
    sums = []
    for i in range(2):
        at = slice(i * rows, (i + 1) * rows)
        mixed = x_ref[at].astype(jnp.float32)
        for term in terms[i]:
            mixed += term[...].astype(jnp.float32)
        mixed_ref[at] = mixed
        hidden_ref[at] = mixed.astype(jnp.bfloat16)
        sums.append(jnp.sum(mixed * mixed, axis=1, keepdims=True))
    column = jnp.broadcast_to(jnp.concatenate(sums, axis=0), (2 * rows, 128))
    square_ref[...] = column.T[: square_ref.shape[0]]


def last_parts(x, prefill, decode):
    rows, columns = x.shape
    flat = pl.BlockSpec((rows, columns), lambda i: (0, 0))
    half = pl.BlockSpec((rows // 2, columns), lambda i: (0, 0))
    return pl.pallas_call(
        last_kernel,
        grid=(1,),
        in_specs=[flat] + [half] * 6,
        out_specs=[flat, flat, pl.BlockSpec((8, rows), lambda i: (0, 0))],
        out_shape=[
            shaped((rows, columns), jnp.float32),
            shaped((rows, columns), jnp.bfloat16),
            shaped((8, rows), jnp.float32),
        ],
        compiler_params=VMEM,
        cost_estimate=cost(4 * x.size, 12 * x.size),
        name="last_parts",
    )(x, *prefill, *decode)


def norm_kernel(width, mixed_ref, square_ref, gain_ref, out_ref):
    inv = lax.rsqrt(square_ref[...].T[:, :1] / width + EPS)
    out_ref[...] = (mixed_ref[...] * inv * gain_ref[...]).astype(jnp.bfloat16)


def norm_out(mixed, squares, gain, width):
    rows, columns = mixed.shape
    return pl.pallas_call(
        functools.partial(norm_kernel, width),
        grid=(1,),
        in_specs=[pl.BlockSpec(a.shape, lambda i: (0, 0)) for a in (mixed, squares, gain)],
        out_specs=pl.BlockSpec((rows, columns), lambda i: (0, 0)),
        out_shape=shaped((rows, columns), jnp.bfloat16),
        compiler_params=VMEM,
        cost_estimate=cost(3 * mixed.size, 6 * mixed.size),
        name="norm_out",
    )(mixed, squares, gain)


def query_kernel(count, first, last, width, blocks, *refs):
    gain_ref, w_ref, *refs = refs
    if not first:
        total_in, squares_in, *refs = refs
    if last:
        cos_ref, sin_ref, *refs = refs
        *pieces, q_ref, inv_ref, scaled, total, squares = refs
    else:
        *pieces, total, squares, scaled = refs
    each = len(pieces) // count
    step = pl.program_id(0)
    rows_each = pieces[0].shape[0]
    gain = gain_ref[...].astype(jnp.float32)

    @pl.when(step == 0)
    def _():
        total[...] = jnp.zeros_like(total) if first else total_in[...]
        squares[...] = jnp.zeros_like(squares) if first else squares_in[...]

    for k in range(count):

        @pl.when(step == k)
        def _(k=k):
            for i in range(each):
                rows = slice(i * rows_each, (i + 1) * rows_each)
                values = pieces[each * k + i][...].astype(jnp.float32)
                squares[rows] += jnp.sum(values * values, axis=1, keepdims=True)
                scaled[rows] = (values * gain).astype(jnp.bfloat16)

    total[...] += dot(scaled[...], w_ref[...])

    if last:

        @pl.when(step == count - 1)
        def _():
            inv = lax.rsqrt(squares[...] / width + EPS)
            inv_ref[...] = inv
            for head in range(q_ref.shape[1] // HEAD_SIZE):
                at = slice(head * HEAD_SIZE, (head + 1) * HEAD_SIZE)
                q_ref[:, at] = turned(total[:, at] * inv, cos_ref[...], sin_ref[...]).astype(
                    jnp.bfloat16
                )


def pick(places, k, blocks):
    block = blocks[places[0]]
    for i, place in enumerate(places[1:], 1):
        block = jnp.where(k == i, blocks[place], block)
    return block


def query_part(places, pieces, gain_row, weight, blocks, sums=None, angles=None, at=0):
    count = len(places)
    rows_each, depth = pieces[0].shape
    rows, width = len(pieces) // count * rows_each, weight.shape[1]
    first, last = sums is None, angles is not None
    whole = lambda shape, at=0: pl.BlockSpec(shape, lambda k, b: (at, 0))
    sum_shapes = [(rows, width), (rows, 1)]
    in_specs = [
        pl.BlockSpec((1, depth), lambda k, b: (0, pick(places, k, b))),
        pl.BlockSpec((depth, width), lambda k, b: (pick(places, k, b), 0)),
    ]
    operands = [gain_row, weight]
    if not first:
        in_specs += [whole(s, at) for s in sum_shapes]
        operands += sums
    scratch = [pltpu.VMEM((rows, depth), jnp.bfloat16)]
    if last:
        in_specs += [whole((rows, HEAD_SIZE))] * 2
        operands += angles
        scratch += [pltpu.VMEM(s, jnp.float32) for s in sum_shapes]
        out_shape = [shaped((rows, width), jnp.bfloat16), shaped((rows, 1), jnp.float32)]
    else:
        out_shape = [shaped(s, jnp.float32) for s in sum_shapes]
    return pl.pallas_call(
        functools.partial(query_kernel, count, first, last, weight.shape[0]),
        grid_spec=pltpu.PrefetchScalarGridSpec(
            num_scalar_prefetch=1,
            grid=(count,),
            in_specs=in_specs + [whole((rows_each, depth))] * len(pieces),
            out_specs=[whole(s) for s in sum_shapes],
            scratch_shapes=scratch,
        ),
        out_shape=out_shape,
        compiler_params=VMEM,
        cost_estimate=cost(2 * count * rows * depth * width, count * depth * width * 4),
        name="query_part",
    )(blocks, *operands, *pieces)


def new_pairs(pairs_ref, inv_ref, cos_ref, sin_ref):
    pairs = (pairs_ref[...] * inv_ref[...]).astype(jnp.bfloat16)
    keys = turned(pairs[:, :HEAD_SIZE].astype(jnp.float32), cos_ref[...], sin_ref[...])
    return keys.astype(jnp.bfloat16), pairs[:, HEAD_SIZE:]


def weight_copies(places, blocks, weight, held, sems):
    columns = held.shape[2]
    return [
        pltpu.make_async_copy(
            weight.at[:, pl.ds(pl.multiple_of(blocks[place] * columns, columns), columns)],
            held.at[i],
            sems.at[i],
        )
        for i, place in enumerate(places)
    ]


def head_columns(ref):
    return [slice(low, low + HEAD_SIZE) for low in range(0, ref.shape[1], HEAD_SIZE)]


def decode_heads(refs, out_ref):
    q_ref, cache_ref, bias_ref, *rest = refs
    keys, values = new_pairs(*rest)
    keys, values = keys.astype(jnp.float32), values.astype(jnp.float32)
    for at in head_columns(out_ref):
        q = q_ref[:, at]
        score = dot_t(q, cache_ref[:, :HEAD_SIZE]) * FACTOR2 + bias_ref[...]
        own = jnp.sum(q.astype(jnp.float32) * keys, axis=1, keepdims=True) * FACTOR2
        peak = jnp.maximum(jnp.max(score, axis=1, keepdims=True), own)
        grown, grown_own = jnp.exp2(score - peak), jnp.exp2(own - peak)
        scale = 1.0 / (jnp.sum(grown, axis=1, keepdims=True) + grown_own)
        context = dot(grown.astype(jnp.bfloat16), cache_ref[:, HEAD_SIZE:])
        out_ref[:, at] = ((context + grown_own * values) * scale).astype(jnp.bfloat16)


def prefill_heads(refs, out_ref):
    q_ref, prefix_ref, bias_ref, *rest = refs
    new_keys, new_values = new_pairs(*rest)
    keys = jnp.concatenate([prefix_ref[:, :HEAD_SIZE], new_keys], axis=0)
    values = jnp.concatenate([prefix_ref[:, HEAD_SIZE:], new_values], axis=0)
    for at in head_columns(out_ref):
        score = dot_t(q_ref[:, at], keys) * FACTOR2 + bias_ref[...]
        grown = jnp.exp2(score - jnp.max(score, axis=1, keepdims=True))
        scale = 1.0 / jnp.sum(grown, axis=1, keepdims=True)
        context = dot(grown.astype(jnp.bfloat16), values) * scale
        out_ref[:, at] = context.astype(jnp.bfloat16)


def context_kernel(heads, places, blocks, *refs):
    if not places:
        heads(refs[:-1], refs[-1])
        return
    *refs, weight, out_ref, first, second, held, sems = refs
    copies = weight_copies(places, blocks, weight, held, sems)
    for copy in copies:
        copy.start()
    heads(refs, out_ref)
    tile = first.shape[1] // 4
    for i, (copy, product) in enumerate(zip(copies, (first, second))):
        copy.wait()
        for low in range(0, product.shape[1], tile):
            at = slice(low, low + tile)
            product[:, at] = dot(out_ref[...], held[i, :, at]).astype(jnp.bfloat16)


def contexts(at, heads, q, pages, bias, pairs, inv, angles, blocks, weight=None, places=()):
    rows, width = bias.shape[0], q.shape[1]
    operands = [q, pages, bias, pairs, inv, *angles]
    in_specs = [pl.BlockSpec(a.shape, lambda i, b: (0, 0)) for a in operands]
    in_specs[0] = pl.BlockSpec((rows, width), lambda i, b: (at, 0))
    in_specs[4] = pl.BlockSpec((rows, 1), lambda i, b: (at, 0))
    out_shape = [shaped((rows, width), jnp.bfloat16)]
    scratch = []
    if places:
        operands.append(weight)
        in_specs.append(pl.BlockSpec(memory_space=pl.ANY))
        columns = weight.shape[1] // RING
        out_shape += [shaped((rows, columns), jnp.bfloat16)] * 2
        scratch = [
            pltpu.VMEM((2, width, columns), jnp.bfloat16),
            pltpu.SemaphoreType.DMA((2,)),
        ]
    return pl.pallas_call(
        functools.partial(context_kernel, heads, places),
        grid_spec=pltpu.PrefetchScalarGridSpec(
            num_scalar_prefetch=1,
            grid=(1,),
            in_specs=in_specs,
            out_specs=[pl.BlockSpec(a.shape, lambda i, b: (0, 0)) for a in out_shape],
            scratch_shapes=scratch,
        ),
        out_shape=out_shape,
        compiler_params=VMEM,
        cost_estimate=cost(8 * rows * width * bias.shape[1], 16 * rows * width),
        name="contexts",
    )(blocks, *operands)


def masks_kernel(
    page_size, request_ref, column_ref, owner_ref, page_ref, pos_ref, prefill_ref, decode_ref
):
    old = owner_ref.shape[1]
    rows = request_ref.shape[0]
    request = request_ref[...]
    prefill_ref[:, :old] = jnp.where(request == owner_ref[...], 0.0, NEGATIVE)
    row = lax.broadcasted_iota(jnp.int32, (rows, rows), 0)
    column = lax.broadcasted_iota(jnp.int32, (rows, rows), 1)
    allowed = (request == column_ref[...]) & (column <= row)
    prefill_ref[:, old:] = jnp.where(allowed, 0.0, NEGATIVE)

    token = lax.broadcasted_iota(jnp.int32, decode_ref.shape, 1)
    page, offset = token // page_size, token % page_size
    times = jnp.zeros(decode_ref.shape, jnp.float32)
    for j in range(page_ref.shape[1]):
        hit = (page == page_ref[:, j : j + 1]) & (offset + j * page_size < pos_ref[...])
        times += jnp.where(hit, 1.0, 0.0)
    decode_ref[...] = jnp.where(times > 0, jnp.log2(jnp.maximum(times, 1.0)), NEGATIVE)


def masks(request, owner, page_table, positions, tokens, page_size):
    rows, decode = request.shape[0], positions.shape[0]
    operands = (
        request[:, None], request[None, :], owner[None, :], page_table, positions[:, None]
    )
    outs = [(rows, owner.shape[0] + rows), (decode, tokens)]
    return pl.pallas_call(
        functools.partial(masks_kernel, page_size),
        grid=(1,),
        in_specs=[pl.BlockSpec(a.shape, lambda i: (0, 0)) for a in operands],
        out_specs=[pl.BlockSpec(a, lambda i: (0, 0)) for a in outs],
        out_shape=[shaped(a, jnp.float32) for a in outs],
        compiler_params=VMEM,
        cost_estimate=cost(20 * decode * tokens, 4 * decode * tokens),
        name="masks",
    )(*operands)


def output_kernel(count, jobs, blocks, *refs):
    contexts, weights, outs = refs[:count], refs[count : -len(jobs)], refs[-len(jobs) :]
    for (c, w), out in zip(jobs, outs):
        out[...] = dot(contexts[c][...], weights[w][...]).astype(jnp.bfloat16)


def output_part(contexts, weight, places, blocks, jobs=None, tiles=4):
    rows, depth = contexts[0].shape
    columns = weight.shape[1] // RING
    tile = columns // tiles
    count = len(contexts)
    jobs = jobs or [(c, w) for w in range(len(places)) for c in range(count)]
    return pl.pallas_call(
        functools.partial(output_kernel, count, tuple(jobs)),
        grid_spec=pltpu.PrefetchScalarGridSpec(
            num_scalar_prefetch=1,
            grid=(tiles,),
            in_specs=[pl.BlockSpec((rows, depth), lambda t, b: (0, 0))] * count
            + [pl.BlockSpec((depth, tile), lambda t, b, p=p: (0, b[p] * tiles + t)) for p in places],
            out_specs=[pl.BlockSpec((rows, tile), lambda t, b: (0, t))] * len(jobs),
        ),
        out_shape=[shaped((rows, columns), jnp.bfloat16)] * len(jobs),
        compiler_params=VMEM,
        cost_estimate=cost(
            2 * len(jobs) * rows * depth * columns, 2 * len(places) * depth * columns
        ),
        name="output_part",
    )(blocks, *contexts, *([weight] * len(places)))


def after(array, *others):
    return lax.optimization_barrier((array, *others))[0]


def hop(ahead, back):
    return lax.ppermute(ahead, "tensor", FORWARD), lax.ppermute(back, "tensor", BACKWARD)


def sum_squares(squares):
    def partner(other):
        return lax.ppermute(squares, "tensor", [(t, t ^ other) for t in range(RING)])

    squares = squares + partner(1)
    return squares + partner(2) + partner(4) + partner(6)


def body(
    inputs,
    entry_gain,
    exit_gain,
    query_weight,
    key_value_matrix,
    output_weight,
    page_pool,
    page_table,
    positions,
    request_lengths,
    prefix_pages,
    source_pages,
    target_pages,
):
    decode = page_table.shape[0]
    prefill = inputs.shape[0] - decode
    page_count, page_size, _ = page_pool.shape
    me = lax.axis_index("tensor")
    width = inputs.shape[1]
    per_device = query_weight.shape[1] // HEAD_SIZE
    group = me * per_device // (QUERY_HEADS // KEY_VALUE_HEADS)
    pair = 2 * HEAD_SIZE

    ring = lax.axis_size("tensor") == RING
    if ring:
        ahead, back = [inputs], [inputs]

        def gather_hop(*others):
            sent = ahead[-1], back[-1]
            if len(ahead) == FAR:
                sent = sent[0][:prefill], sent[1][prefill:]
            if others:
                sent = lax.optimization_barrier((*sent, *others))[:2]
            for pieces, arrived in zip((ahead, back), hop(*sent)):
                pieces.append(arrived)

        gather_hop()
        token = lax.ppermute(inputs[:16, :HEAD_SIZE], "replica", [(0, 1), (1, 0)])
        local = after(inputs, token)
        page_pool, positions, request_lengths, prefix_pages = lax.optimization_barrier(
            (page_pool, positions, request_lengths, prefix_pages, token)
        )[:4]

    own_pool = lax.dynamic_slice_in_dim(page_pool, group * pair, pair, 2)
    peer_pool = lax.ppermute(own_pool, "replica", [(0, 1), (1, 0)])
    prefix = prefix_pages[0]
    page_max = target_pages.shape[2]
    arrived = peer_pool[source_pages.reshape(-1)]
    usable = jnp.arange(page_max, dtype=jnp.int32)[None, :] < prefix[:, None]
    target = jnp.where(usable.reshape(-1), target_pages.reshape(-1), page_count)
    cache = own_pool.at[target].set(arrived, mode="drop").reshape(-1, pair)
    prefix_rows = arrived.reshape(-1, pair)
    slots = jnp.where(usable, jnp.arange(prefix.shape[0], dtype=jnp.int32)[:, None], -1)
    owner = jnp.repeat(slots.reshape(-1), page_size)

    request, span = span_layout(request_lengths[0], prefix, prefill, page_size)
    cosine, sine = tables(jnp.concatenate([span, positions]))
    angles = ((cosine[:prefill], sine[:prefill]), (cosine[prefill:], sine[prefill:]))
    bias = masks(request, owner, page_table, positions, cache.shape[0], page_size)
    gain_row = entry_gain[None, :]

    def attend(which, q, pairs, inv, blocks, *product):
        heads, pages = ((prefill_heads, prefix_rows), (decode_heads, cache))[which]
        return contexts(
            which, heads, q, pages, bias[which], pairs, inv, angles[which], blocks, *product
        )

    exit_row = lax.dynamic_slice_in_dim(exit_gain, me * width, width, 0)
    exit_row = exit_row.astype(jnp.float32)[None, :]

    if ring:
        place = jnp.where(me % 2 == 0, me // 2, RING - 1 - me // 2)
        places = (place + jnp.arange(RING, dtype=jnp.int32)) % RING
        blocks = jnp.where(places < RING // 2, 2 * places, 2 * (RING - places) - 1)
        parts, *moving = pairs_partial(local, gain_row, key_value_matrix, blocks)

        def query(places, sums=None, **more):
            pieces = [back[k] if k < FAR else ahead[RING - k] for k in places]
            return query_part(places, pieces, gain_row, query_weight, blocks, sums, **more)

        def settled(arrived, *others):
            return lax.optimization_barrier((*arrived, *others))[:2]

        arrived = hop(*moving)
        gather_hop()
        moving = add_pairs(*settled(arrived, ahead[1], back[1]), parts, 3, 5)
        sums = query((0, 1, 7))
        arrived = hop(*moving)
        gather_hop(*moving, sums[1])
        sums = query((2, 6), sums)
        moving = add_pairs(
            *settled(arrived, sums[1], cache, *bias, *angles[0], *angles[1]), parts, 2, 6
        )
        arrived = hop(*moving)
        gather_hop(*moving)
        moving = add_pairs(*settled(arrived, ahead[3], back[3]), parts, 1, 7)
        sums = query((3, 5), sums)
        pairs = end_pairs(*settled(hop(*moving), sums[1]), parts)

        q, inv = query_part(
            (FAR,), [ahead[FAR], back[FAR]], gain_row, query_weight, blocks, sums, (cosine, sine)
        )
        prefilled, p4, p5 = attend(0, q, pairs[0], inv, blocks, output_weight, (4, 5))
        p_ahead, p_back = hop(p4, p5)
        decoded, d4, d3 = attend(1, after(q, p4), pairs[1], inv, blocks, output_weight, (4, 3))
        decoded, p_ahead, p_back = lax.optimization_barrier((decoded, p_ahead, p_back))
        d_ahead, d_back = hop(d3, d4)
        both = [prefilled, decoded]
        p3, d5 = output_part(both, output_weight, (3, 5), blocks, [(0, 0), (1, 1)])
        p6, d6, p2, d2 = output_part(both, output_weight, (6, 2), blocks)
        p_ahead, p_back = hop(*add_parts((p_ahead, p_back), (p3, p6)))
        d_ahead, d_back = hop(*add_parts((d_ahead, d_back), (d2, d5)))
        p7, d7, p1, d1 = output_part(both, output_weight, (7, 1), blocks)
        p_ahead, p_back = hop(*add_parts((p_ahead, p_back), (p2, p7)))
        d_ahead, d_back = hop(*add_parts((d_ahead, d_back), (d1, d6)))
        p0, d0 = output_part(both, output_weight, (0,), blocks)
        p_ahead = lax.ppermute(add_parts((p_ahead,), (p1,))[0], "tensor", FORWARD)
        d_back = lax.ppermute(add_parts((d_back,), (d7,))[0], "tensor", BACKWARD)
        mixed, hidden, squares = last_parts(inputs, (p_ahead, p_back, p0), (d_ahead, d_back, d0))
        return hidden, norm_out(mixed, sum_squares(squares), exit_row, exit_gain.shape[0])

    rows = lax.all_gather(inputs, "tensor", axis=1, tiled=True).astype(jnp.float32)
    inv = lax.rsqrt(jnp.mean(rows * rows, axis=1, keepdims=True) + EPS)
    scaled = (rows * inv * entry_gain.astype(jnp.float32)).astype(jnp.bfloat16)
    own = lax.dynamic_slice_in_dim(scaled, me * width, width, 1)
    pairs = lax.psum(dot(own, key_value_matrix), "tensor")
    pairs = lax.dynamic_slice_in_dim(pairs, group * pair, pair, 1)
    q = dot(scaled, query_weight).reshape(-1, per_device, HEAD_SIZE)
    swapped = jnp.roll(q, HEAD_SIZE // 2, 2)
    q = (q * cosine[:, None] + swapped * sine[:, None]).astype(jnp.bfloat16)
    q = q.reshape(-1, per_device * HEAD_SIZE)
    one = jnp.ones_like(inv)
    none = jnp.zeros((1,), jnp.int32)
    context = [
        attend(0, q, pairs[:prefill], one, none)[0],
        attend(1, q, pairs[prefill:], one, none)[0],
    ]
    context = jnp.concatenate(context, axis=0)
    summed = lax.psum_scatter(
        dot(context, output_weight), "tensor", scatter_dimension=1, tiled=True
    )
    mixed = inputs.astype(jnp.float32) + summed
    squares = lax.psum(jnp.sum(mixed * mixed, axis=1), "tensor")[:, None]
    out = mixed * lax.rsqrt(squares / exit_gain.shape[0] + EPS) * exit_row
    return mixed.astype(jnp.bfloat16), out.astype(jnp.bfloat16)


def solution(mesh):
    rows = ("groups", "replica")
    return jax.shard_map(
        body,
        mesh=mesh,
        in_specs=(
            P(rows, "tensor"),
            P(),
            P(),
            P(None, "tensor"),
            P("tensor", None),
            P("tensor", None),
            P(rows, None, None),
            P(rows, None),
            P(rows),
            P(rows, None),
            P(rows, None),
            P(rows, None, None),
            P(rows, None, None),
        ),
        out_specs=(P(rows, "tensor"), P(rows, "tensor")),
        check_vma=False,
    )
```
